32 devices in a mesh: ctx: 8 (over z, x), fsdp: 4 (over y, core).
Axes of the slice: x: 2, y: 2, z: 4, core: 2. Of those that a mesh axis runs over, the one named last changes fastest.
Arguments:
- tokens: bfloat16 [4, 4096, 768], P('fsdp', 'ctx'), may hold values from -6 to 6
- positions: int32 [4, 4096], P('fsdp', 'ctx'), may hold values from 0 to 4095, as said below
- documents: int32 [4, 4096], P('fsdp', 'ctx'), may hold values from 0 to 4, as said below
- ln1_gain: bfloat16 [768], P('fsdp'), may hold values from 0.5 to 1.5
- ln1_bias: bfloat16 [768], P('fsdp'), may hold values from -1 to 1
- w_qkv: bfloat16 [768, 2304], P('fsdp'), may hold values from -0.21875 to 0.21875
- bias_qv: bfloat16 [1536], P('fsdp'), may hold values from -1 to 1
- w_out: bfloat16 [768, 768], P('fsdp'), may hold values from -4 to 4
- bias_out: bfloat16 [768], P('fsdp'), may hold values from -1 to 1
- ln2_gain: bfloat16 [768], P('fsdp'), may hold values from 0.5 to 1.5
- ln2_bias: bfloat16 [768], P('fsdp'), may hold values from -1 to 1
- w_fc: bfloat16 [768, 3072], P('fsdp'), may hold values from -0.21875 to 0.21875
- bias_fc: bfloat16 [3072], P('fsdp'), may hold values from -1 to 1
- w_proj: bfloat16 [3072, 768], P('fsdp'), may hold values from -0.109375 to 0.109375
- bias_proj: bfloat16 [768], P('fsdp'), may hold values from -1 to 1
- cotangent: bfloat16 [4, 4096, 768], P('fsdp', 'ctx'), may hold values from -6 to 6
Outputs:
- block_out: bfloat16 [4, 4096, 768], P('fsdp', 'ctx')
- grad_tokens: bfloat16 [4, 4096, 768], P('fsdp', 'ctx')
- grad_ln1_gain: float32 [768], P('fsdp')
- grad_ln1_bias: float32 [768], P('fsdp')
- grad_w_qkv: float32 [768, 2304], P('fsdp')
- grad_bias_qv: float32 [1536], P('fsdp')
- grad_w_out: float32 [768, 768], P('fsdp')
- grad_bias_out: float32 [768], P('fsdp')
- grad_ln2_gain: float32 [768], P('fsdp')
- grad_ln2_bias: float32 [768], P('fsdp')
- grad_w_fc: float32 [768, 3072], P('fsdp')
- grad_bias_fc: float32 [3072], P('fsdp')
- grad_w_proj: float32 [3072, 768], P('fsdp')
- grad_bias_proj: float32 [768], P('fsdp')
The draws below stay inside these ranges and needn't reach their ends.
Inputs may be any that keep to these rules, and one draw needn't show every extreme that they name: Each device's block of a sequence holds 512 consecutive increasing positions starting at a multiple of 512; the blocks of one sequence hold every position of 0 to 4095 once, in an order that varies from sequence to sequence. `documents`: document numbers never fall as the position rises within a sequence.
All inputs are finite; a program needn't handle non-finite values.
Results may differ from the reference program's by a relative error of at most 0.017.
Values may be sent and summed in bfloat16 or wider, within the bound.
No kernel may reach another device: no remote copies, remote signals or barrier semaphores. Data moves between devices by JAX's collectives and lax.ppermute only.
A program may use at most 192 MiB of HBM per device.

```python
import math
import jax
import jax.numpy as jnp
from jax import lax

D = 768
HEADS = 12
HD = 64
FF = 3072
BLK = 512
SEQS = 4
LEN = 4096


def block_orders(key):
    seq_keys = jax.random.split(key, SEQS)
    return jax.vmap(lambda one_key: jax.random.permutation(one_key, LEN // BLK))(seq_keys)


def placed(orders):
    offsets = jnp.arange(BLK, dtype=jnp.int32)
    return (orders[:, :, None].astype(jnp.int32) * BLK + offsets[None, None, :]).reshape(SEQS, LEN)


def draw_positions(key, part):
    orders = block_orders(key)
    return placed(orders).astype(jnp.int32)


def draw_documents(key, part):
    orders = block_orders(key)
    key = jax.random.fold_in(key, 23)
    where_at = placed(orders)
    lower_end = (jnp.minimum(orders[:, 0], orders[:, -1]) * BLK).astype(jnp.int32)
    upper_end = ((jnp.maximum(orders[:, 0], orders[:, -1]) + 1) * BLK).astype(jnp.int32)
    key_low, key_high = jax.random.split(key)
    cut_low = jax.random.randint(key_low, (SEQS,), 0, lower_end + 1)
    cut_high = jax.random.randint(key_high, (SEQS,), upper_end, LEN + 1)
    doc_ids = (where_at >= cut_low[:, None]).astype(jnp.int32) + (where_at >= lower_end[:, None]).astype(jnp.int32) + (where_at >= upper_end[:, None]).astype(jnp.int32) + (where_at >= cut_high[:, None]).astype(jnp.int32)
    return doc_ids.astype(jnp.int32)


def shard_levels(stream_key, dims, pieces, low, largest):
    loudness = 1.0
    for axis_at, shards_of in pieces:
        heights = jax.random.uniform(jax.random.fold_in(jax.random.fold_in(stream_key, 6), axis_at), (shards_of,), jnp.float32, low / len(pieces), largest / len(pieces))
        loudness = loudness * jnp.repeat(jnp.exp(heights), dims[axis_at] // shards_of).reshape((-1,) + (1,) * (len(dims) - 1 - axis_at))
    return loudness


def centred(key, extent, scale, most, pieces=(), kind=jnp.bfloat16):
    entries = scale * jax.random.normal(key, extent, jnp.float32)
    if pieces:
        entries = entries * shard_levels(key, extent, pieces, -0.22, 0.18)
    return jnp.clip(entries, -most, most).astype(kind)


def setup_inputs(seed: int = 0) -> dict:
    streams_of = jax.random.split(jax.random.key(seed), 17)
    return {
        "tokens": centred(streams_of[0], (SEQS, LEN, D), 1.0, 6.0, ((0, 4), (1, 8))),
        "positions": draw_positions(jax.random.fold_in(streams_of[16], 71), 0),
        "documents": draw_documents(jax.random.fold_in(streams_of[16], 71), 0),
        "ln1_gain": jnp.clip(1.0 + 0.1 * jax.random.normal(streams_of[3], (D,), jnp.float32), 0.5, 1.5).astype(jnp.bfloat16),
        "ln1_bias": centred(streams_of[4], (D,), 0.2, 1.0, ((0, 4),)),
        "w_qkv": centred(streams_of[5], (D, 3 * D), D ** -0.5, 0.21875, ((0, 4),)),
        "bias_qv": centred(streams_of[6], (2 * D,), 0.2, 1.0, ((0, 4),)),
        "w_out": centred(streams_of[7], (D, D), 2 ** -0.5, 4.0, ((0, 4),)),
        "bias_out": centred(streams_of[8], (D,), 0.2, 1.0, ((0, 4),)),
        "ln2_gain": jnp.clip(1.0 + 0.1 * jax.random.normal(streams_of[9], (D,), jnp.float32), 0.5, 1.5).astype(jnp.bfloat16),
        "ln2_bias": centred(streams_of[10], (D,), 0.2, 1.0, ((0, 4),)),
        "w_fc": centred(streams_of[11], (D, FF), D ** -0.5, 0.21875, ((0, 4),)),
        "bias_fc": centred(streams_of[12], (FF,), 0.2, 1.0, ((0, 4),)),
        "w_proj": centred(streams_of[13], (FF, D), FF ** -0.5, 0.109375, ((0, 4),)),
        "bias_proj": centred(streams_of[14], (D,), 0.2, 1.0, ((0, 4),)),
        "cotangent": centred(streams_of[15], (SEQS, LEN, D), 1.0, 6.0, ((0, 4), (1, 8))),
    }


EPS = 1e-05
NEG = -1e+30
PRECISE = lax.Precision.HIGHEST

@jax.custom_vjp
def low(v):
    return lax.optimization_barrier(v.astype(jnp.bfloat16)).astype(jnp.float32)

@jax.custom_vjp
def low_back(v):
    return v

def low_keep(v):
    return (low(v), None)

def low_pass(kept, grad):
    return (grad,)

def back_keep(v):
    return (v, None)

def back_low(kept, grad):
    return (low(grad),)
low.defvjp(low_keep, low_pass)
low_back.defvjp(back_keep, back_low)

def both_ways(v):
    return low_back(low(v))

def norm_rows(v, gain, shift):
    centered = v - lax.optimization_barrier(jnp.mean(v, -1, keepdims=True))
    inverse = lax.rsqrt(lax.optimization_barrier(jnp.mean(centered * centered, -1, keepdims=True)) + EPS)
    return centered * inverse * gain + shift

def attend(q, k, v, place, doc_ids):
    n_rows = q.shape[0]
    block_rows = math.gcd(512, n_rows)
    n_heads = q.shape[1]
    score_scale = float(q.shape[2]) ** (-0.5)

    def query_block(element):
        q_block, place_block, doc_block = element
        s = low_back(jnp.einsum('qhc,khc->hqk', q_block, k, precision=PRECISE) * score_scale)
        visible = (place[None, :] <= place_block[:, None]) & (doc_ids[None, :] == doc_block[:, None])
        s = jnp.where(visible[None], s, NEG)
        row_max = lax.optimization_barrier(jnp.max(s, -1, keepdims=True))
        weights_raw = jnp.where(visible[None], jnp.exp(s - row_max), 0.0)
        softmax_w = low(weights_raw / lax.optimization_barrier(jnp.sum(weights_raw, -1, keepdims=True)))
        return jnp.einsum('hqk,khc->qhc', softmax_w, v, precision=PRECISE)
    blocks = lax.map(jax.checkpoint(query_block), (q.reshape(n_rows // block_rows, block_rows, n_heads, -1), place.reshape(-1, block_rows), doc_ids.reshape(-1, block_rows)))
    return blocks.reshape(n_rows, -1)

def layer(params, x, place, doc_ids):
    g_one, b_one, w_qkv, b_qv, w_out, b_out, g_two, b_two, w_fc, b_fc, w_proj, b_proj = params
    model_width = x.shape[1]
    n_rows = x.shape[0]
    h_one = low(norm_rows(x, g_one, b_one))
    bias_all = jnp.concatenate([b_qv[:model_width], jnp.zeros_like(b_qv[:model_width]), b_qv[model_width:]])
    qkv = jnp.dot(h_one, w_qkv, precision=PRECISE) + bias_all
    q = both_ways(qkv[:, :model_width]).reshape(n_rows, HEADS, HD)
    k = both_ways(qkv[:, model_width:2 * model_width]).reshape(n_rows, HEADS, HD)
    v = both_ways(qkv[:, 2 * model_width:]).reshape(n_rows, HEADS, HD)
    attended = both_ways(attend(q, k, v, place, doc_ids))
    branch = low_back(jnp.dot(attended, w_out, precision=PRECISE) + b_out)
    x_two = x + branch
    h_two = low(norm_rows(x_two, g_two, b_two))
    f = low_back(jnp.dot(h_two, w_fc, precision=PRECISE) + b_fc)
    u = low(jax.nn.gelu(f, approximate=True))
    mlp_out = low_back(jnp.dot(u, w_proj, precision=PRECISE) + b_proj)
    return x_two + mlp_out

def reference(tokens, positions, documents, ln1_gain, ln1_bias, w_qkv, bias_qv, w_out, bias_out, ln2_gain, ln2_bias, w_fc, bias_fc, w_proj, bias_proj, cotangent):
    params = tuple((w.astype(jnp.float32) for w in (ln1_gain, ln1_bias, w_qkv, bias_qv, w_out, bias_out, ln2_gain, ln2_bias, w_fc, bias_fc, w_proj, bias_proj)))

    def per_sequence(running, element):
        x_seq, place, doc_ids, cot_seq = element

        def forward(weights, inputs):
            return layer(weights, inputs, place, doc_ids)
        result, pullback = jax.vjp(forward, params, x_seq.astype(jnp.float32))
        grad_params, grad_input = pullback(cot_seq.astype(jnp.float32))
        running = tuple((a + b for a, b in zip(running, grad_params)))
        return (running, (result.astype(jnp.bfloat16), grad_input.astype(jnp.bfloat16)))
    zero_grads = tuple((jnp.zeros_like(w) for w in params))
    running, outputs = lax.scan(per_sequence, zero_grads, (tokens, positions, documents, cotangent))
    block_out, grad_tokens = outputs
    return (block_out, grad_tokens, running[0], running[1], running[2], running[3], running[4], running[5], running[6], running[7], running[8], running[9], running[10], running[11])
```

```python
import functools

import jax
import jax.numpy as jnp
from jax import lax
from jax.experimental import pallas as pl
from jax.experimental.pallas import tpu as pltpu
from jax.sharding import PartitionSpec as P

HEADS = 12
HEAD_GROUPS = 2 * HEADS // 3

EPS = 1e-05
NEG = -1e30


def norm_stats(v):
    centered = v - jnp.mean(v, -1, keepdims=True)
    inverse = lax.rsqrt(jnp.mean(centered * centered, -1, keepdims=True) + EPS)
    return (centered * inverse, inverse)


def norm_back(grad_h, normed, inverse, gain):
    grad_normed = grad_h * gain
    return inverse * (
        grad_normed
        - jnp.mean(grad_normed, -1, keepdims=True)
        - normed * jnp.mean(grad_normed * normed, -1, keepdims=True)
    )


def dot_nt(a, b):
    return lax.dot_general(a, b, (((1,), (1,)), ((), ())), preferred_element_type=jnp.float32)


def dot_tn(a, b):
    return lax.dot_general(a, b, (((0,), (0,)), ((), ())), preferred_element_type=jnp.float32)


def dot_nn(a, b):
    return lax.dot_general(a, b, (((1,), (0,)), ((), ())), preferred_element_type=jnp.float32)


def own_lanes(rows, width, side):
    lane = lax.broadcasted_iota(jnp.int32, (rows, width), 1)
    return (lane >= width // 2) == (side == 1)


def load_rows(window_ref, block, padded_ref, side, scale):
    rows, width = window_ref.shape[1:]
    half = rows // 2
    f32 = jnp.float32
    whole = window_ref[block].astype(f32) * scale
    padded_ref[block, :rows, :] = jnp.where(own_lanes(rows, width, side), whole, 0.0).astype(jnp.bfloat16)
    start = pl.multiple_of(side * half, half)
    part = window_ref[block, pl.ds(start, half), :].astype(f32) * scale
    padded_ref[block, rows:, :] = jnp.where(own_lanes(half, width, side), 0.0, part).astype(jnp.bfloat16)


def store_rows(window_ref, block, value, side):
    rows, width = window_ref.shape[1:]
    half = rows // 2
    own = own_lanes(rows, width, side)
    row = lax.broadcasted_iota(jnp.int32, (rows, width), 0)
    mine = (row >= half) == (side == 1)
    shared = jnp.concatenate([value[rows:], value[rows:]], 0)
    shared = jnp.where(mine, shared, 0.0)
    window_ref[block] = jnp.where(own, value[:rows], shared).astype(window_ref.dtype)


def column_chunks(total):
    size = 256 if total % 256 == 0 else total
    return [(at, size) for at in range(0, total, size)]


def visible_pairs(key_meta_ref, query_meta_ref, block, at, size):
    key_place, key_doc = key_meta_ref[0, :, 0:1], key_meta_ref[0, :, 1:2]
    query_place = query_meta_ref[block, 0:1, at : at + size]
    query_doc = query_meta_ref[block, 1:2, at : at + size]
    return (key_place <= query_place) & (key_doc == query_doc)


def attend_kernel(
    kind_ref, side_ref, q_ref, k_ref, v_ref, query_meta_ref, key_meta_ref,
    window_ref, out_ref, log_ref, rows_ref, max_ref, sum_ref, *, scale,
):
    f32 = jnp.float32
    blocks, width, total = out_ref.shape
    key_block = pl.program_id(0)
    side = side_ref[0]

    @pl.when(key_block == 0)
    def _():
        @pl.loop(0, blocks)
        def _(block):
            load_rows(q_ref, block, rows_ref, side, scale)
            max_ref[block] = jnp.full((1, total), NEG, f32)
            sum_ref[block] = jnp.zeros((1, total), f32)
            out_ref[block] = jnp.zeros((width, total), f32)

    def work(block, partial):
        keys, values = k_ref[0], v_ref[0]
        for at, size in column_chunks(total):
            span = slice(at, at + size)
            s = dot_nt(keys, rows_ref[block, span, :])
            if partial:
                visible = visible_pairs(key_meta_ref, query_meta_ref, block, at, size)
                s = jnp.where(visible, s, NEG)
            old_max = max_ref[block, :, span]
            new_max = jnp.maximum(old_max, jnp.max(s, 0, keepdims=True))
            weights = jnp.exp(s - new_max)
            if partial:
                weights = jnp.where(visible, weights, 0.0)
            factor = jnp.exp(old_max - new_max)
            max_ref[block, :, span] = new_max
            sum_ref[block, :, span] = sum_ref[block, :, span] * factor + jnp.sum(weights, 0, keepdims=True)
            added = dot_tn(values, weights.astype(jnp.bfloat16))
            out_ref[block, :, span] = out_ref[block, :, span] * factor + added

    @pl.loop(0, blocks)
    def _(block):
        kind = kind_ref[block * blocks + key_block]

        @pl.when(kind == 1)
        def _():
            work(block, False)

        @pl.when(kind == 2)
        def _():
            work(block, True)

    @pl.when(key_block == blocks - 1)
    def _():
        @pl.loop(0, blocks)
        def _(block):
            total_weight = sum_ref[block]
            out = out_ref[block] / total_weight
            out_ref[block] = out
            log_ref[block] = max_ref[block] + jnp.log(total_weight)
            store_rows(window_ref, block, out.T, side)


def attend_back_kernel(
    kind_ref, side_ref, q_ref, k_ref, v_ref, query_meta_ref, key_meta_ref, grad_ref, out_ref, log_ref,
    grad_q_ref, grad_k_ref, grad_v_ref, rows_ref, grad_rows_ref, delta_ref, sum_q_ref, sum_k_ref, sum_v_ref,
    *, scale,
):
    f32, bf16 = jnp.float32, jnp.bfloat16
    blocks, width, total = out_ref.shape
    key_block = pl.program_id(0)
    side = side_ref[0]

    @pl.when(key_block == 0)
    def _():
        @pl.loop(0, blocks)
        def _(block):
            load_rows(q_ref, block, rows_ref, side, scale)
            load_rows(grad_ref, block, grad_rows_ref, side, 1.0)
            grad_rows = grad_rows_ref[block].astype(f32).T
            delta_ref[block] = jnp.sum(grad_rows * out_ref[block], 0, keepdims=True)
            sum_q_ref[block] = jnp.zeros((width, total), f32)

    sum_k_ref[...] = jnp.zeros_like(sum_k_ref)
    sum_v_ref[...] = jnp.zeros_like(sum_v_ref)

    def work(block, partial):
        keys, values = k_ref[0], v_ref[0]
        for at, size in column_chunks(total):
            span = slice(at, at + size)
            q_rows = rows_ref[block, span, :]
            grad_rows = grad_rows_ref[block, span, :]
            prob = jnp.exp(dot_nt(keys, q_rows) - log_ref[block, :, span])
            if partial:
                visible = visible_pairs(key_meta_ref, query_meta_ref, block, at, size)
                prob = jnp.where(visible, prob, 0.0)
            grad_prob = dot_nt(values, grad_rows)
            sum_v_ref[...] += dot_nn(prob.astype(bf16), grad_rows)
            grad_score = (prob * (grad_prob - delta_ref[block, :, span])).astype(bf16)
            sum_k_ref[...] += dot_nn(grad_score, q_rows)
            sum_q_ref[block, :, span] += dot_tn(keys, grad_score)

    @pl.loop(0, blocks)
    def _(block):
        kind = kind_ref[block * blocks + key_block]

        @pl.when(kind == 1)
        def _():
            work(block, False)

        @pl.when(kind == 2)
        def _():
            work(block, True)

    grad_k_ref[0] = sum_k_ref[...].astype(bf16)
    grad_v_ref[0] = sum_v_ref[...].astype(bf16)

    @pl.when(key_block == blocks - 1)
    def _():
        @pl.loop(0, blocks)
        def _(block):
            store_rows(grad_q_ref, block, sum_q_ref[block].T * scale, side)


def whole_spec(shape, at=0):
    return pl.BlockSpec(shape, lambda i, *_: (0,) * (len(shape) - 1) + (at,))


def attention_calls(blocks, query_len, key_len, width, lanes, scale):
    f32, bf16 = jnp.float32, jnp.bfloat16
    total = query_len + query_len // 2
    shape = jax.ShapeDtypeStruct
    q_spec = whole_spec((blocks, query_len, width), lanes[0])
    block_spec = lambda at: pl.BlockSpec((1, key_len, width), lambda i, *_: (i, 0, at))
    metas = [
        whole_spec((blocks, 2, total)),
        pl.BlockSpec((1, key_len, 2), lambda i, *_: (i, 0, 0)),
    ]
    operands = [q_spec, block_spec(lanes[1]), block_spec(lanes[2])] + metas
    window = whole_spec((blocks, query_len, width))
    columns = whole_spec((blocks, width, total))
    logs = whole_spec((blocks, 1, total))
    params = pltpu.CompilerParams(dimension_semantics=("arbitrary",), vmem_limit_bytes=56 * 1024 * 1024)
    pairs = blocks * (blocks + 1) // 2
    product = 2 * total * key_len * width * pairs
    forward = pl.pallas_call(
        functools.partial(attend_kernel, scale=scale),
        grid_spec=pltpu.PrefetchScalarGridSpec(
            num_scalar_prefetch=2,
            grid=(blocks,),
            in_specs=operands,
            out_specs=[window, columns, logs],
            scratch_shapes=[
                pltpu.VMEM((blocks, total, width), bf16),
                pltpu.VMEM((blocks, 1, total), f32),
                pltpu.VMEM((blocks, 1, total), f32),
            ],
        ),
        out_shape=[
            shape((blocks, query_len, width), bf16),
            shape((blocks, width, total), f32),
            shape((blocks, 1, total), f32),
        ],
        compiler_params=params,
        cost_estimate=pl.CostEstimate(
            flops=8 * product, bytes_accessed=16 << 20, transcendentals=total * key_len * pairs
        ),
        name="attend",
    )
    backward = pl.pallas_call(
        functools.partial(attend_back_kernel, scale=scale),
        grid_spec=pltpu.PrefetchScalarGridSpec(
            num_scalar_prefetch=2,
            grid=(blocks,),
            in_specs=operands + [window, columns, logs],
            out_specs=[window, block_spec(0), block_spec(0)],
            scratch_shapes=[
                pltpu.VMEM((blocks, total, width), bf16),
                pltpu.VMEM((blocks, total, width), bf16),
                pltpu.VMEM((blocks, 1, total), f32),
                pltpu.VMEM((blocks, width, total), f32),
                pltpu.VMEM((key_len, width), f32),
                pltpu.VMEM((key_len, width), f32),
            ],
        ),
        out_shape=[
            shape((blocks, query_len, width), bf16),
            shape((blocks, key_len, width), bf16),
            shape((blocks, key_len, width), bf16),
        ],
        compiler_params=params,
        cost_estimate=pl.CostEstimate(
            flops=20 * product, bytes_accessed=24 << 20, transcendentals=total * key_len * pairs
        ),
        name="attend_back",
    )
    return forward, backward


def swapped(pieces, axis):
    length = len(pieces)
    return [pieces[0]] + [
        lax.ppermute(pieces[k], axis, [(i, i ^ k) for i in range(length)]) for k in range(1, length)
    ]


def per_device(
    tokens,
    positions,
    documents,
    ln1_gain,
    ln1_bias,
    w_qkv,
    bias_qv,
    w_out,
    bias_out,
    ln2_gain,
    ln2_bias,
    w_fc,
    bias_fc,
    w_proj,
    bias_proj,
    cotangent,
):
    f32 = jnp.float32
    bf16 = jnp.bfloat16
    seq_count, block_len, model_width = tokens.shape
    head_dim = model_width // HEADS
    width = 2 * head_dim
    score_scale = float(head_dim) ** (-0.5)
    cycle_len = lax.axis_size("ctx")
    owners = lax.axis_size("fsdp")
    me = lax.axis_index("ctx")
    pieces = cycle_len // HEAD_GROUPS
    pair_wise = pieces == 1
    group, piece = me % HEAD_GROUPS, me // HEAD_GROUPS
    side = group % 2
    query_len = block_len // pieces
    half = query_len // 2
    starts = [3 * head_dim * (j // 2) + head_dim * (j % 2) for j in range(HEAD_GROUPS)]
    forward_call, backward_call = attention_calls(
        cycle_len, query_len, block_len, width, (0, 1, 2) if pair_wise else (0, 0, 1), score_scale
    )

    order = jnp.bitwise_xor(me, jnp.arange(cycle_len)) if pair_wise else jnp.arange(cycle_len)
    ids = lax.all_gather(jnp.concatenate([positions, documents], 0), "ctx", axis=0)[order]
    places, docs = ids[:, 0], ids[:, 1]
    first_place, last_place = places[:, 0], places[:, -1]
    first_doc, last_doc = docs[:, 0], docs[:, -1]
    hidden = (
        (first_place[None, :] > last_place[:, None])
        | (last_doc[None, :] < first_doc[:, None])
        | (first_doc[None, :] > last_doc[:, None])
    )
    full = (
        (last_place[None, :] <= first_place[:, None])
        & (first_doc[None, :] == last_doc[:, None])
        & (last_doc[None, :] == first_doc[:, None])
    )
    kinds = jnp.where(hidden, 0, jnp.where(full, 1, 2)).astype(jnp.int32).reshape(-1)
    own_ids = lax.dynamic_slice_in_dim(ids, piece * query_len, query_len, 2)
    shared_ids = lax.dynamic_slice_in_dim(own_ids, side * half, half, 2)
    query_meta = jnp.concatenate([own_ids, shared_ids], 2)
    key_meta = jnp.swapaxes(ids, 1, 2)
    side_arg = side.reshape(1).astype(jnp.int32)

    def windows(rows):
        return jnp.stack([rows[:, at : at + width] for at in starts])

    def block_at(stacked, j):
        return lax.dynamic_index_in_dim(stacked, j, 0, keepdims=False)

    def query_pieces(stacked):
        return stacked.reshape(HEAD_GROUPS, pieces, query_len, -1).swapaxes(0, 1).reshape(cycle_len, query_len, -1)

    def over_pieces(stacked):
        return jnp.tile(stacked, (pieces, 1, 1))

    def scattered(stacked):
        if pair_wise:
            return jnp.stack(swapped([block_at(stacked, me ^ k) for k in range(cycle_len)], "ctx"))
        return lax.all_to_all(stacked, "ctx", 0, 0, tiled=True)

    def returned(stacked):
        if pair_wise:
            back = jnp.stack(swapped([stacked[k] for k in range(cycle_len)], "ctx"))
            return jnp.stack([block_at(back, me ^ j) for j in range(cycle_len)])
        return lax.all_to_all(stacked, "ctx", 0, 0, tiled=True)

    def joined_queries(back):
        back = back.reshape(pieces, HEAD_GROUPS, query_len, width).swapaxes(0, 1)
        back = back.reshape(HEAD_GROUPS // 2, 2, pieces, 2, half, width)
        lower = back[:, 0, :, 0, :, head_dim:]
        upper = back[:, 1, :, 1, :, :head_dim]
        shared = jnp.stack([lower, upper], 2)
        parts = [back[:, 0, ..., :head_dim], shared, back[:, 1, ..., head_dim:]]
        parts = [part.reshape(HEAD_GROUPS // 2, block_len, head_dim) for part in parts]
        return jnp.concatenate([parts[m][g] for g in range(HEAD_GROUPS // 2) for m in range(3)], 1)

    def joined_keys(back):
        back = back.reshape(pieces, HEAD_GROUPS // 2, 2, block_len, width).astype(f32).sum(0)
        shared = back[:, 0, :, head_dim:] + back[:, 1, :, :head_dim]
        parts = [back[:, 0, :, :head_dim], shared, back[:, 1, :, head_dim:]]
        return jnp.concatenate([parts[m][g] for g in range(HEAD_GROUPS // 2) for m in range(3)], 1).astype(bf16)

    vectors = (ln1_gain, ln1_bias, bias_qv, bias_out, ln2_gain, ln2_bias, bias_fc, bias_proj)
    vector_sizes = [v.size for v in vectors]
    gathered = lax.all_gather(jnp.concatenate(vectors), "fsdp", axis=0).astype(f32)
    cuts = [sum(vector_sizes[:i]) for i in range(len(vectors) + 1)]
    gain_one, shift_one, bqv_all, bout_all, gain_two, shift_two, bfc_all, bproj_all = [
        gathered[:, cuts[i] : cuts[i + 1]].reshape(-1) for i in range(len(vectors))
    ]
    wqkv_all = lax.all_gather(w_qkv, "fsdp", axis=0, tiled=True)
    x = tokens.astype(f32).reshape(-1, model_width)
    normed_one, inverse_one = norm_stats(x)
    h_one = (normed_one * gain_one + shift_one).astype(bf16)
    bias_all = jnp.concatenate(
        [bqv_all[:model_width], jnp.zeros((model_width,), f32), bqv_all[model_width:]]
    )
    qkv = (jnp.dot(h_one, wqkv_all, preferred_element_type=f32) + bias_all).astype(bf16)
    q_windows, k_windows, v_windows = [
        windows(qkv[:, i * model_width : (i + 1) * model_width]) for i in range(3)
    ]
    if pair_wise:
        taken = scattered(jnp.concatenate([q_windows, k_windows, v_windows], -1))
        operands = (taken, taken, taken)
    else:
        taken_q = scattered(query_pieces(q_windows))
        taken_kv = scattered(over_pieces(jnp.concatenate([k_windows, v_windows], -1)))
        operands = (taken_q, taken_kv, taken_kv)
    operands = (kinds, side_arg) + operands + (query_meta, key_meta)
    wfc_all = lax.all_gather(w_fc, "fsdp", axis=0, tiled=True)
    late = lax.all_gather(jnp.concatenate([w_proj, w_out], 0), "fsdp", axis=0)
    wproj_all = late[:, : w_proj.shape[0]].reshape(-1, model_width)
    wout_all = late[:, w_proj.shape[0] :].reshape(-1, model_width)
    out_windows, out_columns, log_total = forward_call(*operands)
    attended_low = joined_queries(returned(out_windows))
    x_two = x + jnp.dot(attended_low, wout_all, preferred_element_type=f32) + bout_all
    normed_two, inverse_two = norm_stats(x_two)
    h_two = (normed_two * gain_two + shift_two).astype(bf16)
    pre_act = jnp.dot(h_two, wfc_all, preferred_element_type=f32) + bfc_all
    activated, gelu_pull = jax.vjp(lambda t: jax.nn.gelu(t, approximate=True), pre_act)
    activated_low = activated.astype(bf16)
    result = x_two + jnp.dot(activated_low, wproj_all, preferred_element_type=f32) + bproj_all
    block_out = result.astype(bf16).reshape(tokens.shape)
    cot_rows = cotangent.reshape(-1, model_width)
    grad_y = cot_rows.astype(f32)
    grad_bproj = jnp.sum(grad_y, 0)
    grad_act = jnp.einsum("td,fd->tf", cot_rows, wproj_all, preferred_element_type=f32)
    grad_pre = gelu_pull(grad_act)[0].astype(bf16)
    grad_bfc = jnp.sum(grad_pre.astype(f32), 0)
    grad_h_two = jnp.einsum("tf,df->td", grad_pre, wfc_all, preferred_element_type=f32)
    grad_g_two = jnp.sum(grad_h_two * normed_two, 0)
    grad_b_two = jnp.sum(grad_h_two, 0)
    grad_x_two = grad_y + norm_back(grad_h_two, normed_two, inverse_two, gain_two)
    grad_branch = grad_x_two.astype(bf16)
    grad_bout = jnp.sum(grad_branch.astype(f32), 0)
    grad_att = jnp.einsum("te,de->td", grad_branch, wout_all, preferred_element_type=f32).astype(bf16)
    taken_grad = scattered(query_pieces(windows(grad_att)))

    def reduced(grad):
        own = lax.psum_scatter(grad, "fsdp", scatter_dimension=0, tiled=True)
        mine = lax.psum_scatter(own, "ctx", scatter_dimension=0, tiled=True)
        return lax.all_gather(mine, "ctx", axis=0, tiled=True).astype(f32)

    grad_wproj = jnp.einsum("tf,td->fd", activated_low, cot_rows, preferred_element_type=f32).astype(bf16)
    grad_wfc = jnp.einsum("td,tf->df", h_two, grad_pre, preferred_element_type=f32).astype(bf16)
    grad_wout = jnp.einsum("td,te->de", attended_low, grad_branch, preferred_element_type=f32).astype(bf16)
    reduced_wproj = reduced(grad_wproj)
    reduced_wfc = reduced(grad_wfc)
    reduced_wout = reduced(grad_wout)

    grad_q_windows, grad_k_windows, grad_v_windows = backward_call(
        *operands, taken_grad, out_columns, log_total
    )
    if pair_wise:
        back = returned(jnp.concatenate([grad_q_windows, grad_k_windows, grad_v_windows], -1))
        back_q, back_k, back_v = [back[..., i * width : (i + 1) * width] for i in range(3)]
    else:
        back_q = returned(grad_q_windows)
        back_kv = returned(jnp.concatenate([grad_k_windows, grad_v_windows], -1))
        back_k, back_v = back_kv[..., :width], back_kv[..., width:]
    grad_q_low, grad_k_low, grad_v_low = joined_queries(back_q), joined_keys(back_k), joined_keys(back_v)
    grad_qkv = jnp.concatenate([grad_q_low, grad_k_low, grad_v_low], -1)
    grad_bqv = jnp.concatenate(
        [jnp.sum(grad_q_low.astype(f32), 0), jnp.sum(grad_v_low.astype(f32), 0)]
    )
    grad_wqkv = jnp.einsum("td,te->de", h_one, grad_qkv, preferred_element_type=f32).astype(bf16)
    grad_h_one = jnp.einsum("te,de->td", grad_qkv, wqkv_all, preferred_element_type=f32)
    grad_g_one = jnp.sum(grad_h_one * normed_one, 0)
    grad_b_one = jnp.sum(grad_h_one, 0)
    grad_x = grad_x_two + norm_back(grad_h_one, normed_one, inverse_one, gain_one)
    grad_tokens = grad_x.astype(bf16).reshape(tokens.shape)

    vector_grads = (grad_g_one, grad_b_one, grad_bqv, grad_bout, grad_g_two, grad_b_two, grad_bfc, grad_bproj)
    packed = jnp.concatenate([grad.reshape(owners, -1) for grad in vector_grads], 1).astype(bf16)
    own_rows = w_qkv.shape[0]
    extra = -(-packed.shape[1] // (own_rows * 128)) * 128
    packed = jnp.pad(packed, ((0, 0), (0, own_rows * extra - packed.shape[1])))
    packed = packed.reshape(owners * own_rows, extra)
    last = reduced(jnp.concatenate([grad_wqkv, packed], 1))
    reduced_wqkv = last[:, : w_qkv.shape[1]]
    reduced_vectors = last[:, w_qkv.shape[1] :].reshape(-1)
    pieces_of = [reduced_vectors[cuts[i] : cuts[i + 1]] for i in range(len(vectors))]
    g_one, b_one, g_bqv, g_bout, g_two, b_two, g_bfc, g_bproj = pieces_of
    return (
        block_out,
        grad_tokens,
        g_one,
        b_one,
        reduced_wqkv,
        g_bqv,
        reduced_wout,
        g_bout,
        g_two,
        b_two,
        reduced_wfc,
        g_bfc,
        reduced_wproj,
        g_bproj,
    )


def solution(mesh):
    return jax.shard_map(
        per_device,
        mesh=mesh,
        in_specs=(
            P("fsdp", "ctx", None),
            P("fsdp", "ctx"),
            P("fsdp", "ctx"),
            P("fsdp"),
            P("fsdp"),
            P("fsdp", None),
            P("fsdp"),
            P("fsdp", None),
            P("fsdp"),
            P("fsdp"),
            P("fsdp"),
            P("fsdp", None),
            P("fsdp"),
            P("fsdp", None),
            P("fsdp"),
            P("fsdp", "ctx", None),
        ),
        out_specs=(
            P("fsdp", "ctx", None),
            P("fsdp", "ctx", None),
            P("fsdp"),
            P("fsdp"),
            P("fsdp", None),
            P("fsdp"),
            P("fsdp", None),
            P("fsdp"),
            P("fsdp"),
            P("fsdp"),
            P("fsdp", None),
            P("fsdp"),
            P("fsdp", None),
            P("fsdp"),
        ),
        check_vma=False,
    )
```

```python
import functools

import jax
import jax.numpy as jnp
from jax import lax
from jax.experimental import pallas as pl
from jax.experimental.pallas import tpu as pltpu
from jax.sharding import PartitionSpec as P

HEADS = 12
HEAD_GROUPS = 2 * HEADS // 3

EPS = 1e-05
NEG = -1e30


def norm_stats(v):
    centered = v - jnp.mean(v, -1, keepdims=True)
    inverse = lax.rsqrt(jnp.mean(centered * centered, -1, keepdims=True) + EPS)
    return (centered * inverse, inverse)


def norm_back(grad_h, normed, inverse, gain):
    grad_normed = grad_h * gain
    return inverse * (
        grad_normed
        - jnp.mean(grad_normed, -1, keepdims=True)
        - normed * jnp.mean(grad_normed * normed, -1, keepdims=True)
    )


def dot_nt(a, b):
    return lax.dot_general(a, b, (((1,), (1,)), ((), ())), preferred_element_type=jnp.float32)


def dot_tn(a, b):
    return lax.dot_general(a, b, (((0,), (0,)), ((), ())), preferred_element_type=jnp.float32)


def dot_nn(a, b):
    return lax.dot_general(a, b, (((1,), (0,)), ((), ())), preferred_element_type=jnp.float32)


def own_lanes(rows, width, side):
    lane = lax.broadcasted_iota(jnp.int32, (rows, width), 1)
    return (lane >= width // 2) == (side == 1)


def load_rows(window_ref, block, padded_ref, side, scale):
    rows, width = window_ref.shape[1:]
    half = rows // 2
    f32 = jnp.float32
    whole = window_ref[block].astype(f32) * scale
    padded_ref[block, :rows, :] = jnp.where(own_lanes(rows, width, side), whole, 0.0).astype(jnp.bfloat16)
    start = pl.multiple_of(side * half, half)
    part = window_ref[block, pl.ds(start, half), :].astype(f32) * scale
    padded_ref[block, rows:, :] = jnp.where(own_lanes(half, width, side), 0.0, part).astype(jnp.bfloat16)


def store_rows(window_ref, block, value, side):
    rows, width = window_ref.shape[1:]
    half = rows // 2
    own = own_lanes(rows, width, side)
    row = lax.broadcasted_iota(jnp.int32, (rows, width), 0)
    mine = (row >= half) == (side == 1)
    shared = jnp.concatenate([value[rows:], value[rows:]], 0)
    shared = jnp.where(mine, shared, 0.0)
    window_ref[block] = jnp.where(own, value[:rows], shared).astype(window_ref.dtype)


def column_chunks(total):
    size = 256 if total % 256 == 0 else total
    return [(at, size) for at in range(0, total, size)]


def visible_pairs(key_meta_ref, query_meta_ref, block, at, size):
    key_place, key_doc = key_meta_ref[0, :, 0:1], key_meta_ref[0, :, 1:2]
    query_place = query_meta_ref[block, 0:1, at : at + size]
    query_doc = query_meta_ref[block, 1:2, at : at + size]
    return (key_place <= query_place) & (key_doc == query_doc)


def attend_kernel(
    kind_ref, side_ref, q_ref, k_ref, v_ref, query_meta_ref, key_meta_ref,
    window_ref, out_ref, log_ref, rows_ref, max_ref, sum_ref, *, scale,
):
    f32 = jnp.float32
    blocks, width, total = out_ref.shape
    key_block = pl.program_id(0)
    side = side_ref[0]

    @pl.when(key_block == 0)
    def _():
        @pl.loop(0, blocks)
        def _(block):
            load_rows(q_ref, block, rows_ref, side, scale)
            max_ref[block] = jnp.full((1, total), NEG, f32)
            sum_ref[block] = jnp.zeros((1, total), f32)
            out_ref[block] = jnp.zeros((width, total), f32)

    def work(block, partial):
        keys, values = k_ref[0], v_ref[0]
        for at, size in column_chunks(total):
            span = slice(at, at + size)
            s = dot_nt(keys, rows_ref[block, span, :])
            if partial:
                visible = visible_pairs(key_meta_ref, query_meta_ref, block, at, size)
                s = jnp.where(visible, s, NEG)
            old_max = max_ref[block, :, span]
            new_max = jnp.maximum(old_max, jnp.max(s, 0, keepdims=True))
            weights = jnp.exp(s - new_max)
            if partial:
                weights = jnp.where(visible, weights, 0.0)
            factor = jnp.exp(old_max - new_max)
            max_ref[block, :, span] = new_max
            sum_ref[block, :, span] = sum_ref[block, :, span] * factor + jnp.sum(weights, 0, keepdims=True)
            added = dot_tn(values, weights.astype(jnp.bfloat16))
            out_ref[block, :, span] = out_ref[block, :, span] * factor + added

    @pl.loop(0, blocks)
    def _(block):
        kind = kind_ref[block * blocks + key_block]

        @pl.when(kind == 1)
        def _():
            work(block, False)

        @pl.when(kind == 2)
        def _():
            work(block, True)

    @pl.when(key_block == blocks - 1)
    def _():
        @pl.loop(0, blocks)
        def _(block):
            total_weight = sum_ref[block]
            out = out_ref[block] / total_weight
            out_ref[block] = out
            log_ref[block] = max_ref[block] + jnp.log(total_weight)
            store_rows(window_ref, block, out.T, side)


def attend_back_kernel(
    kind_ref, side_ref, q_ref, k_ref, v_ref, query_meta_ref, key_meta_ref, grad_ref, out_ref, log_ref,
    grad_q_ref, grad_k_ref, grad_v_ref, rows_ref, grad_rows_ref, delta_ref, sum_q_ref, sum_k_ref, sum_v_ref,
    *, scale,
):
    f32, bf16 = jnp.float32, jnp.bfloat16
    blocks, width, total = out_ref.shape
    key_block = pl.program_id(0)
    side = side_ref[0]

    @pl.when(key_block == 0)
    def _():
        @pl.loop(0, blocks)
        def _(block):
            load_rows(q_ref, block, rows_ref, side, scale)
            load_rows(grad_ref, block, grad_rows_ref, side, 1.0)
            grad_rows = grad_rows_ref[block].astype(f32).T
            delta_ref[block] = jnp.sum(grad_rows * out_ref[block], 0, keepdims=True)
            sum_q_ref[block] = jnp.zeros((width, total), f32)

    sum_k_ref[...] = jnp.zeros_like(sum_k_ref)
    sum_v_ref[...] = jnp.zeros_like(sum_v_ref)

    def work(block, partial):
        keys, values = k_ref[0], v_ref[0]
        for at, size in column_chunks(total):
            span = slice(at, at + size)
            q_rows = rows_ref[block, span, :]
            grad_rows = grad_rows_ref[block, span, :]
            prob = jnp.exp(dot_nt(keys, q_rows) - log_ref[block, :, span])
            if partial:
                visible = visible_pairs(key_meta_ref, query_meta_ref, block, at, size)
                prob = jnp.where(visible, prob, 0.0)
            grad_prob = dot_nt(values, grad_rows)
            sum_v_ref[...] += dot_nn(prob.astype(bf16), grad_rows)
            grad_score = (prob * (grad_prob - delta_ref[block, :, span])).astype(bf16)
            sum_k_ref[...] += dot_nn(grad_score, q_rows)
            sum_q_ref[block, :, span] += dot_tn(keys, grad_score)

    @pl.loop(0, blocks)
    def _(block):
        kind = kind_ref[block * blocks + key_block]

        @pl.when(kind == 1)
        def _():
            work(block, False)

        @pl.when(kind == 2)
        def _():
            work(block, True)

    grad_k_ref[0] = sum_k_ref[...].astype(bf16)
    grad_v_ref[0] = sum_v_ref[...].astype(bf16)

    @pl.when(key_block == blocks - 1)
    def _():
        @pl.loop(0, blocks)
        def _(block):
            store_rows(grad_q_ref, block, sum_q_ref[block].T * scale, side)


def whole_spec(shape, at=0):
    return pl.BlockSpec(shape, lambda i, *_: (0,) * (len(shape) - 1) + (at,))


def attention_calls(blocks, query_len, key_len, width, lanes, scale, earlier):
    f32, bf16 = jnp.float32, jnp.bfloat16
    total = query_len + query_len // 2
    shape = jax.ShapeDtypeStruct
    q_spec = whole_spec((blocks, query_len, width), lanes[0])
    block_spec = lambda at: pl.BlockSpec((1, key_len, width), lambda i, *_: (i, 0, at))
    metas = [
        whole_spec((blocks, 2, total)),
        pl.BlockSpec((1, key_len, 2), lambda i, *_: (i, 0, 0)),
    ]
    operands = [q_spec, block_spec(lanes[1]), block_spec(lanes[2])] + metas
    window = whole_spec((blocks, query_len, width))
    columns = whole_spec((blocks, width, total))
    logs = whole_spec((blocks, 1, total))
    params = pltpu.CompilerParams(dimension_semantics=("arbitrary",), vmem_limit_bytes=56 * 1024 * 1024)
    pairs = blocks * (blocks + 1) // 2
    product = 2 * total * key_len * width * pairs
    forward = pl.pallas_call(
        functools.partial(attend_kernel, scale=scale),
        grid_spec=pltpu.PrefetchScalarGridSpec(
            num_scalar_prefetch=2,
            grid=(blocks,),
            in_specs=operands,
            out_specs=[window, columns, logs],
            scratch_shapes=[
                pltpu.VMEM((blocks, total, width), bf16),
                pltpu.VMEM((blocks, 1, total), f32),
                pltpu.VMEM((blocks, 1, total), f32),
            ],
        ),
        out_shape=[
            shape((blocks, query_len, width), bf16),
            shape((blocks, width, total), f32),
            shape((blocks, 1, total), f32),
        ],
        compiler_params=params,
        cost_estimate=pl.CostEstimate(
            flops=8 * product, bytes_accessed=16 << 20, transcendentals=total * key_len * pairs
        ),
        name="attend",
    )
    backward = pl.pallas_call(
        leading(functools.partial(attend_back_kernel, scale=scale), 10, earlier),
        grid_spec=pltpu.PrefetchScalarGridSpec(
            num_scalar_prefetch=2,
            grid=(blocks,),
            in_specs=operands + [window, columns, logs] + [ANY_SPEC] * earlier,
            out_specs=[window, block_spec(0), block_spec(0)],
            scratch_shapes=[
                pltpu.VMEM((blocks, total, width), bf16),
                pltpu.VMEM((blocks, total, width), bf16),
                pltpu.VMEM((blocks, 1, total), f32),
                pltpu.VMEM((blocks, width, total), f32),
                pltpu.VMEM((key_len, width), f32),
                pltpu.VMEM((key_len, width), f32),
            ],
        ),
        out_shape=[
            shape((blocks, query_len, width), bf16),
            shape((blocks, key_len, width), bf16),
            shape((blocks, key_len, width), bf16),
        ],
        compiler_params=params,
        cost_estimate=pl.CostEstimate(
            flops=20 * product, bytes_accessed=24 << 20, transcendentals=total * key_len * pairs
        ),
        name="attend_back",
    )
    return forward, backward


def mixed(left, right):
    width = left.shape[1]
    lane = lax.broadcasted_iota(jnp.int32, left.shape, 1)
    return jnp.where(lane < width // 2, pltpu.roll(left, width // 2, 1), pltpu.roll(right, width // 2, 1))


def leading(kernel, count, earlier):
    return lambda *refs: kernel(*refs[:count], *refs[count + earlier :])


def split_kernel(me_ref, rows_ref, *refs, carried):
    outs, windows_ref = refs[carried : carried + HEAD_GROUPS], refs[-1]
    for source, target in zip(refs[:carried], refs[carried + HEAD_GROUPS : -1]):
        target[...] = source[...]
    width = 128
    parts = windows_ref.shape[2] // width
    per_part = rows_ref.shape[1] // parts
    for i in range(parts):
        for t in range(HEAD_GROUPS // 4):
            at = i * per_part + 3 * width * t
            low, middle, high = [
                rows_ref[:, at + m * width : at + (m + 1) * width].astype(jnp.float32) for m in range(3)
            ]
            for g, value in enumerate((low, mixed(low, middle), mixed(middle, high), high)):
                windows_ref[4 * t + g, :, i * width : (i + 1) * width] = value.astype(windows_ref.dtype)
    for k, out in enumerate(outs):
        out[...] = windows_ref[jnp.bitwise_xor(me_ref[0], k)]


def join_kernel(me_ref, *refs):
    f32 = jnp.float32
    ins, (rows_ref, sums_ref, windows_ref) = refs[:HEAD_GROUPS], refs[HEAD_GROUPS:]
    width = 128
    parts = windows_ref.shape[2] // width
    per_part = rows_ref.shape[1] // parts
    for k, value_ref in enumerate(ins):
        windows_ref[jnp.bitwise_xor(me_ref[0], k)] = value_ref[...]
    for i in range(parts):
        span = slice(i * width, (i + 1) * width)
        for t in range(HEAD_GROUPS // 4):
            a, b, c, d = [windows_ref[4 * t + g, :, span].astype(f32) for g in range(4)]
            lower = lax.broadcasted_iota(jnp.int32, a.shape, 1) < width // 2
            b, c = pltpu.roll(b, width // 2, 1), pltpu.roll(c, width // 2, 1)
            values = (
                a + jnp.where(lower, 0.0, b),
                jnp.where(lower, b, c),
                jnp.where(lower, c, 0.0) + d,
            )
            for m, value in enumerate(values):
                at = i * per_part + (3 * t + m) * width
                value = value.astype(rows_ref.dtype)
                rows_ref[:, at : at + width] = value
                sums_ref[:, at : at + width] = jnp.sum(value.astype(f32), 0, keepdims=True)


SMEM_SPEC = pl.BlockSpec(memory_space=pltpu.SMEM)
ANY_SPEC = pl.BlockSpec(memory_space=pl.ANY)
VMEM_SPEC = pl.BlockSpec(memory_space=pltpu.VMEM)
LOCAL = pltpu.CompilerParams(vmem_limit_bytes=48 * 1024 * 1024)


def split_rows(me, rows, parts, carried):
    count = rows.shape[0]
    columns = 128 * parts
    outs = pl.pallas_call(
        functools.partial(split_kernel, carried=len(carried)),
        in_specs=[SMEM_SPEC] + [VMEM_SPEC] * (1 + len(carried)),
        out_specs=[VMEM_SPEC] * (HEAD_GROUPS + len(carried)),
        out_shape=[jax.ShapeDtypeStruct((count, columns), rows.dtype)] * HEAD_GROUPS
        + [jax.ShapeDtypeStruct(array.shape, array.dtype) for array in carried],
        scratch_shapes=[pltpu.VMEM((HEAD_GROUPS, count, columns), rows.dtype)],
        compiler_params=LOCAL,
        cost_estimate=pl.CostEstimate(flops=0, bytes_accessed=4 * rows.size * 2, transcendentals=0),
        name="split_rows",
    )(me, rows, *carried)
    return outs[:HEAD_GROUPS], outs[HEAD_GROUPS:]


def add_kernel(kept_ref, received_ref, sum_ref):
    total = kept_ref[...].astype(jnp.float32) + received_ref[...].astype(jnp.float32)
    sum_ref[...] = total.astype(sum_ref.dtype)


def added_after(kept, received, earlier):
    return pl.pallas_call(
        leading(add_kernel, 2, len(earlier)),
        in_specs=[VMEM_SPEC] * 2 + [ANY_SPEC] * len(earlier),
        out_specs=VMEM_SPEC,
        out_shape=jax.ShapeDtypeStruct(kept.shape, kept.dtype),
        compiler_params=LOCAL,
        cost_estimate=pl.CostEstimate(flops=0, bytes_accessed=6 * kept.size, transcendentals=0),
        name="added_after",
    )(kept, received, *earlier)


def pack_kernel(*refs):
    arrays, outs = refs[:-HEAD_GROUPS], refs[-HEAD_GROUPS:]
    for k, out in enumerate(outs):
        for i, array in enumerate(arrays):
            width = array.shape[2]
            out[:, i * width : (i + 1) * width] = array[k]


def pack_rows(arrays, earlier=()):
    blocks, count, width = arrays[0].shape
    shape = jax.ShapeDtypeStruct((count, width * len(arrays)), arrays[0].dtype)
    return pl.pallas_call(
        leading(pack_kernel, len(arrays), len(earlier)),
        in_specs=[VMEM_SPEC] * len(arrays) + [ANY_SPEC] * len(earlier),
        out_specs=[VMEM_SPEC] * blocks,
        out_shape=[shape] * blocks,
        compiler_params=LOCAL,
        cost_estimate=pl.CostEstimate(flops=0, bytes_accessed=4 * blocks * shape.size, transcendentals=0),
        name="pack_rows",
    )(*arrays, *earlier)


def join_rows(me, pieces, model_width, earlier=()):
    count, columns = pieces[0].shape
    total = model_width * columns // 128
    return pl.pallas_call(
        leading(join_kernel, 1 + HEAD_GROUPS, len(earlier)),
        in_specs=[SMEM_SPEC] + [VMEM_SPEC] * HEAD_GROUPS + [ANY_SPEC] * len(earlier),
        out_specs=[VMEM_SPEC, VMEM_SPEC],
        out_shape=[
            jax.ShapeDtypeStruct((count, total), pieces[0].dtype),
            jax.ShapeDtypeStruct((1, total), jnp.float32),
        ],
        scratch_shapes=[pltpu.VMEM((HEAD_GROUPS, count, columns), pieces[0].dtype)],
        compiler_params=LOCAL,
        cost_estimate=pl.CostEstimate(flops=0, bytes_accessed=4 * count * total * 2, transcendentals=0),
        name="join_rows",
    )(me, *pieces, *earlier)


def swapped(pieces, axis):
    length = len(pieces)
    return [pieces[0]] + [
        lax.ppermute(pieces[k], axis, [(i, i ^ k) for i in range(length)]) for k in range(1, length)
    ]


def per_device(
    tokens,
    positions,
    documents,
    ln1_gain,
    ln1_bias,
    w_qkv,
    bias_qv,
    w_out,
    bias_out,
    ln2_gain,
    ln2_bias,
    w_fc,
    bias_fc,
    w_proj,
    bias_proj,
    cotangent,
):
    f32 = jnp.float32
    bf16 = jnp.bfloat16
    seq_count, block_len, model_width = tokens.shape
    head_dim = model_width // HEADS
    width = 2 * head_dim
    score_scale = float(head_dim) ** (-0.5)
    cycle_len = lax.axis_size("ctx")
    owners = lax.axis_size("fsdp")
    me = lax.axis_index("ctx")
    pieces = cycle_len // HEAD_GROUPS
    pair_wise = pieces == 1
    group, piece = me % HEAD_GROUPS, me // HEAD_GROUPS
    side = group % 2
    query_len = block_len // pieces
    half = query_len // 2
    starts = [3 * head_dim * (j // 2) + head_dim * (j % 2) for j in range(HEAD_GROUPS)]
    forward_call, backward_call = attention_calls(
        cycle_len, query_len, block_len, width, (0, 1, 2) if pair_wise else (0, 0, 1), score_scale,
        4 if pair_wise else 0,
    )

    def exchange(value, axis, by):
        return lax.ppermute(value, axis, [(i, i ^ by) for i in range(lax.axis_size(axis))])

    ids = jnp.stack([positions[0], documents[0]])[None]
    if pair_wise:
        by = 1
        while by < cycle_len:
            ids = jnp.concatenate([ids, exchange(ids, "ctx", by)], 0)
            by *= 2
    else:
        ids = lax.all_gather(ids[0], "ctx", axis=0)
    def metas(ids):
        places, docs = ids[:, 0], ids[:, 1]
        first_place, last_place = places[:, 0], places[:, -1]
        first_doc, last_doc = docs[:, 0], docs[:, -1]
        hidden = (
            (first_place[None, :] > last_place[:, None])
            | (last_doc[None, :] < first_doc[:, None])
            | (first_doc[None, :] > last_doc[:, None])
        )
        full = (
            (last_place[None, :] <= first_place[:, None])
            & (first_doc[None, :] == last_doc[:, None])
            & (last_doc[None, :] == first_doc[:, None])
        )
        kinds = jnp.where(hidden, 0, jnp.where(full, 1, 2)).astype(jnp.int32).reshape(-1)
        own_ids = lax.dynamic_slice_in_dim(ids, piece * query_len, query_len, 2)
        shared_ids = lax.dynamic_slice_in_dim(own_ids, side * half, half, 2)
        return kinds, jnp.concatenate([own_ids, shared_ids], 2), jnp.swapaxes(ids, 1, 2)

    side_arg = side.reshape(1).astype(jnp.int32)

    def windows(rows):
        return jnp.stack([rows[:, at : at + width] for at in starts])

    def block_at(stacked, j):
        return lax.dynamic_index_in_dim(stacked, j, 0, keepdims=False)

    def query_pieces(stacked):
        return stacked.reshape(HEAD_GROUPS, pieces, query_len, -1).swapaxes(0, 1).reshape(cycle_len, query_len, -1)

    def over_pieces(stacked):
        return jnp.tile(stacked, (pieces, 1, 1))

    def all_to_all(stacked):
        return lax.all_to_all(stacked, "ctx", 0, 0, tiled=True)

    def joined_queries(back):
        back = back.reshape(pieces, HEAD_GROUPS, query_len, width).swapaxes(0, 1)
        back = back.reshape(HEAD_GROUPS // 2, 2, pieces, 2, half, width)
        lower = back[:, 0, :, 0, :, head_dim:]
        upper = back[:, 1, :, 1, :, :head_dim]
        shared = jnp.stack([lower, upper], 2)
        parts = [back[:, 0, ..., :head_dim], shared, back[:, 1, ..., head_dim:]]
        parts = [part.reshape(HEAD_GROUPS // 2, block_len, head_dim) for part in parts]
        return jnp.concatenate([parts[m][g] for g in range(HEAD_GROUPS // 2) for m in range(3)], 1)

    def joined_keys(back):
        back = back.reshape(pieces, HEAD_GROUPS // 2, 2, block_len, width).astype(f32).sum(0)
        shared = back[:, 0, :, head_dim:] + back[:, 1, :, :head_dim]
        parts = [back[:, 0, :, :head_dim], shared, back[:, 1, :, head_dim:]]
        return jnp.concatenate([parts[m][g] for g in range(HEAD_GROUPS // 2) for m in range(3)], 1).astype(bf16)

    vectors = (ln1_gain, ln1_bias, bias_qv, bias_out, ln2_gain, ln2_bias, bias_fc, bias_proj)
    vector_sizes = [v.size for v in vectors]
    gathered = lax.all_gather(jnp.concatenate(vectors), "fsdp", axis=0).astype(f32)
    cuts = [sum(vector_sizes[:i]) for i in range(len(vectors) + 1)]
    gain_one, shift_one, bqv_all, bout_all, gain_two, shift_two, bfc_all, bproj_all = [
        gathered[:, cuts[i] : cuts[i + 1]].reshape(-1) for i in range(len(vectors))
    ]
    wqkv_all = lax.all_gather(w_qkv, "fsdp", axis=0, tiled=True)
    wfc_all = lax.all_gather(w_fc, "fsdp", axis=0, tiled=True)
    late = lax.all_gather(jnp.concatenate([w_proj, w_out], 0), "fsdp", axis=0)
    wproj_all = late[:, : w_proj.shape[0]].reshape(-1, model_width)
    wout_all = late[:, w_proj.shape[0] :].reshape(-1, model_width)
    me_arg = me.reshape(1).astype(jnp.int32)
    x = tokens.astype(f32).reshape(-1, model_width)
    normed_one, inverse_one = norm_stats(x)
    h_one = (normed_one * gain_one + shift_one).astype(bf16)
    bias_all = jnp.concatenate(
        [bqv_all[:model_width], jnp.zeros((model_width,), f32), bqv_all[model_width:]]
    )
    qkv = (jnp.dot(h_one, wqkv_all, preferred_element_type=f32) + bias_all).astype(bf16)
    if pair_wise:
        parts, (ids,) = split_rows(me_arg, qkv, 3, (ids,))
        taken = jnp.stack(swapped(parts, "ctx"))
        operands = (taken, taken, taken)
    else:
        q_windows, k_windows, v_windows = [
            windows(qkv[:, i * model_width : (i + 1) * model_width]) for i in range(3)
        ]
        taken_q = all_to_all(query_pieces(q_windows))
        taken_kv = all_to_all(over_pieces(jnp.concatenate([k_windows, v_windows], -1)))
        operands = (taken_q, taken_kv, taken_kv)
    kinds, query_meta, key_meta = metas(ids)
    operands = (kinds, side_arg) + operands + (query_meta, key_meta)
    out_windows, out_columns, log_total = forward_call(*operands)
    cot_rows = cotangent.reshape(-1, model_width)
    grad_act = jnp.einsum("td,fd->tf", cot_rows, wproj_all, preferred_element_type=f32)
    if pair_wise:
        back = swapped([out_windows[k] for k in range(cycle_len)], "ctx")
        attended_low, _ = join_rows(me_arg, back, model_width, (wproj_all, wout_all, grad_act))
    else:
        attended_low = joined_queries(all_to_all(out_windows))
    x_two = x + jnp.dot(attended_low, wout_all, preferred_element_type=f32) + bout_all
    normed_two, inverse_two = norm_stats(x_two)
    h_two = (normed_two * gain_two + shift_two).astype(bf16)
    pre_act = jnp.dot(h_two, wfc_all, preferred_element_type=f32) + bfc_all
    activated, gelu_pull = jax.vjp(lambda t: jax.nn.gelu(t, approximate=True), pre_act)
    activated_low = activated.astype(bf16)
    result = x_two + jnp.dot(activated_low, wproj_all, preferred_element_type=f32) + bproj_all
    block_out = result.astype(bf16).reshape(tokens.shape)
    grad_y = cot_rows.astype(f32)
    grad_bproj = jnp.sum(grad_y, 0)
    grad_pre = gelu_pull(grad_act)[0].astype(bf16)
    grad_bfc = jnp.sum(grad_pre.astype(f32), 0)
    grad_h_two = jnp.einsum("tf,df->td", grad_pre, wfc_all, preferred_element_type=f32)
    grad_g_two = jnp.sum(grad_h_two * normed_two, 0)
    grad_b_two = jnp.sum(grad_h_two, 0)
    grad_x_two = grad_y + norm_back(grad_h_two, normed_two, inverse_two, gain_two)
    grad_branch = grad_x_two.astype(bf16)
    grad_bout = jnp.sum(grad_branch.astype(f32), 0)
    grad_att = jnp.einsum("te,de->td", grad_branch, wout_all, preferred_element_type=f32).astype(bf16)
    row, column = me // 2, me % 2
    chip, core = lax.axis_index("fsdp") // 2, lax.axis_index("fsdp") % 2
    rows_apart = cycle_len // 2

    def pick(value, j, axis):
        return lax.dynamic_index_in_dim(value, j, axis, keepdims=False)

    def added(kept, *others):
        total = kept.astype(f32)
        for other in others:
            total = total + other.astype(f32)
        return total.astype(bf16)

    def product(left, right):
        grad = jnp.einsum("tr,tc->rc", left, right, preferred_element_type=f32).astype(bf16)
        return grad.reshape(owners // 2, 2, -1, grad.shape[1])

    def over_cores(grad):
        return added(pick(grad, core, 1), exchange(pick(grad, 1 - core, 1), "fsdp", 1))

    def first_parts(a, b):
        b = b.reshape(2, rows_apart, 2, -1, b.shape[-1])
        return (pick(a, chip, 0), pick(b, column, 2)), (pick(a, 1 - chip, 0), pick(b, 1 - column, 2))

    def second_parts(kept, sent, earlier=()):
        a = added_after(kept[0], exchange(sent[0], "fsdp", 2), earlier)
        b = added_after(kept[1], exchange(sent[1], "ctx", 1), earlier)
        a = a.reshape(rows_apart, 2, -1, a.shape[-1])
        return (pick(a, column, 1), pick(b, chip, 0)), (pick(a, 1 - column, 1), pick(b, 1 - chip, 0))

    def third_parts(kept, sent, earlier=()):
        a = added_after(kept[0], exchange(sent[0], "ctx", 1), earlier)
        return a, added_after(kept[1], exchange(sent[1], "fsdp", 2), earlier)

    def last_sum(value):
        return added(
            pick(value, row, 0), *[exchange(pick(value, row ^ k, 0), "ctx", 2 * k) for k in range(1, rows_apart)]
        )

    def spread(mine):
        around = jnp.stack([mine] + [exchange(mine, "ctx", 2 * k) for k in range(1, rows_apart)])
        around = jnp.stack([pick(around, row ^ j, 0) for j in range(rows_apart)])
        both = jnp.stack([around, exchange(around, "ctx", 1)])
        both = jnp.stack([pick(both, column ^ j, 0) for j in range(2)], 1)
        return both.reshape(-1, mine.shape[-1])

    def over_ctx(pair):
        own = added(pick(pair, chip, 0), exchange(pick(pair, 1 - chip, 0), "fsdp", 2))
        mine = lax.psum_scatter(own, "ctx", scatter_dimension=0, tiled=True)
        return lax.all_gather(mine, "ctx", axis=0, tiled=True)

    def early_sums(cot_rows, h_two, attended_low):
        early = [
            over_cores(product(left, right))
            for left, right in ((activated_low, cot_rows), (h_two, grad_pre), (attended_low, grad_branch))
        ]
        return early[0], jnp.concatenate(early[1:], -1)

    if pair_wise:
        parts, carried = split_rows(me_arg, grad_att, 1, (cot_rows, h_two, attended_low))
        taken_grad = jnp.stack(swapped(parts, "ctx"))
        early = first_parts(*early_sums(*carried))
        earlier = (*early[0], *early[1])
    else:
        taken_grad = all_to_all(query_pieces(windows(grad_att)))
        early = [over_ctx(pair) for pair in early_sums(cot_rows, h_two, attended_low)]
        earlier = ()

    grad_q_windows, grad_k_windows, grad_v_windows = backward_call(
        *operands, taken_grad, out_columns, log_total, *earlier
    )
    if pair_wise:
        back = swapped(pack_rows((grad_q_windows, grad_k_windows, grad_v_windows)), "ctx")
        early = second_parts(*early, (grad_q_windows,))
        grad_qkv, grad_sums = join_rows(me_arg, back, model_width)
        early = [spread(last_sum(value)) for value in third_parts(*early, (grad_qkv,))]
        grad_sums = grad_sums[0]
    else:
        back_q = all_to_all(grad_q_windows)
        back_kv = all_to_all(jnp.concatenate([grad_k_windows, grad_v_windows], -1))
        grad_k_low, grad_v_low = joined_keys(back_kv[..., :width]), joined_keys(back_kv[..., width:])
        grad_qkv = jnp.concatenate([joined_queries(back_q), grad_k_low, grad_v_low], -1)
        grad_sums = jnp.sum(grad_qkv.astype(f32), 0)
    grad_bqv = jnp.concatenate([grad_sums[:model_width], grad_sums[2 * model_width :]])
    grad_h_one = jnp.einsum("te,de->td", grad_qkv, wqkv_all, preferred_element_type=f32)
    grad_g_one = jnp.sum(grad_h_one * normed_one, 0)
    grad_b_one = jnp.sum(grad_h_one, 0)
    grad_x = grad_x_two + norm_back(grad_h_one, normed_one, inverse_one, gain_one)
    grad_tokens = grad_x.astype(bf16).reshape(tokens.shape)

    vector_grads = (grad_g_one, grad_b_one, grad_bqv, grad_bout, grad_g_two, grad_b_two, grad_bfc, grad_bproj)
    packed = jnp.concatenate([grad.reshape(owners, -1) for grad in vector_grads], 1).astype(bf16)
    own_rows = w_qkv.shape[0]
    extra = -(-packed.shape[1] // (own_rows * 128)) * 128
    packed = jnp.pad(packed, ((0, 0), (0, own_rows * extra - packed.shape[1])))
    packed = packed.reshape(owners // 2, 2, own_rows, extra)
    last = over_cores(jnp.concatenate([product(h_one, grad_qkv), packed], -1))
    if pair_wise:
        cut = w_qkv.shape[1] // 256 * 128
        last = third_parts(*second_parts(*first_parts(last[..., :cut], last[..., cut:])))
        last = spread(last_sum(jnp.concatenate(last, -1)))
    else:
        last = over_ctx(last)
    last = last.astype(f32)
    early = [value.astype(f32) for value in early]
    reduced_wproj = early[0]
    reduced_wfc, reduced_wout = early[1][:, : w_fc.shape[1]], early[1][:, w_fc.shape[1] :]
    reduced_wqkv = last[:, : w_qkv.shape[1]]
    reduced_vectors = last[:, w_qkv.shape[1] :].reshape(-1)
    pieces_of = [reduced_vectors[cuts[i] : cuts[i + 1]] for i in range(len(vectors))]
    g_one, b_one, g_bqv, g_bout, g_two, b_two, g_bfc, g_bproj = pieces_of
    return (
        block_out,
        grad_tokens,
        g_one,
        b_one,
        reduced_wqkv,
        g_bqv,
        reduced_wout,
        g_bout,
        g_two,
        b_two,
        reduced_wfc,
        g_bfc,
        reduced_wproj,
        g_bproj,
    )


def solution(mesh):
    return jax.shard_map(
        per_device,
        mesh=mesh,
        in_specs=(
            P("fsdp", "ctx", None),
            P("fsdp", "ctx"),
            P("fsdp", "ctx"),
            P("fsdp"),
            P("fsdp"),
            P("fsdp", None),
            P("fsdp"),
            P("fsdp", None),
            P("fsdp"),
            P("fsdp"),
            P("fsdp"),
            P("fsdp", None),
            P("fsdp"),
            P("fsdp", None),
            P("fsdp"),
            P("fsdp", "ctx", None),
        ),
        out_specs=(
            P("fsdp", "ctx", None),
            P("fsdp", "ctx", None),
            P("fsdp"),
            P("fsdp"),
            P("fsdp", None),
            P("fsdp"),
            P("fsdp", None),
            P("fsdp"),
            P("fsdp"),
            P("fsdp"),
            P("fsdp", None),
            P("fsdp"),
            P("fsdp", None),
            P("fsdp"),
        ),
        check_vma=False,
    )
```

```python
import functools

import jax
import jax.numpy as jnp
from jax import lax
from jax.experimental import pallas as pl
from jax.experimental.pallas import tpu as pltpu
from jax.sharding import PartitionSpec as P

HEADS = 12
HEAD_GROUPS = 2 * HEADS // 3

EPS = 1e-05
NEG = -1e30


def norm_stats(v):
    centered = v - jnp.mean(v, -1, keepdims=True)
    inverse = lax.rsqrt(jnp.mean(centered * centered, -1, keepdims=True) + EPS)
    return (centered * inverse, inverse)


def norm_back(grad_h, normed, inverse, gain):
    grad_normed = grad_h * gain
    return inverse * (
        grad_normed
        - jnp.mean(grad_normed, -1, keepdims=True)
        - normed * jnp.mean(grad_normed * normed, -1, keepdims=True)
    )


def dot_nt(a, b):
    return lax.dot_general(a, b, (((1,), (1,)), ((), ())), preferred_element_type=jnp.float32)


def dot_tn(a, b):
    return lax.dot_general(a, b, (((0,), (0,)), ((), ())), preferred_element_type=jnp.float32)


def dot_nn(a, b):
    return lax.dot_general(a, b, (((1,), (0,)), ((), ())), preferred_element_type=jnp.float32)


def own_lanes(rows, width, side):
    lane = lax.broadcasted_iota(jnp.int32, (rows, width), 1)
    return (lane >= width // 2) == (side == 1)


def load_rows(window_ref, block, padded_ref, side, scale):
    rows, width = window_ref.shape[1:]
    half = rows // 2
    f32 = jnp.float32
    whole = window_ref[block].astype(f32) * scale
    padded_ref[block, :rows, :] = jnp.where(own_lanes(rows, width, side), whole, 0.0).astype(jnp.bfloat16)
    start = pl.multiple_of(side * half, half)
    part = window_ref[block, pl.ds(start, half), :].astype(f32) * scale
    padded_ref[block, rows:, :] = jnp.where(own_lanes(half, width, side), 0.0, part).astype(jnp.bfloat16)


def store_rows(window_ref, block, value, side):
    rows, width = window_ref.shape[1:]
    half = rows // 2
    own = own_lanes(rows, width, side)
    row = lax.broadcasted_iota(jnp.int32, (rows, width), 0)
    mine = (row >= half) == (side == 1)
    shared = jnp.concatenate([value[rows:], value[rows:]], 0)
    shared = jnp.where(mine, shared, 0.0)
    window_ref[block] = jnp.where(own, value[:rows], shared).astype(window_ref.dtype)


def column_chunks(total):
    size = 256 if total % 256 == 0 else total
    return [(at, size) for at in range(0, total, size)]


def visible_pairs(key_meta_ref, query_meta_ref, block, span):
    key_place, key_doc = key_meta_ref[0, :, 0:1], key_meta_ref[0, :, 1:2]
    query_place, query_doc = query_meta_ref[block, 0:1, span], query_meta_ref[block, 1:2, span]
    return (key_place <= query_place) & (key_doc == query_doc)


def attend_kernel(
    kind_ref, side_ref, q_ref, k_ref, v_ref, query_meta_ref, key_meta_ref,
    window_ref, out_ref, log_ref, rows_ref, max_ref, sum_ref, *, scale,
):
    f32 = jnp.float32
    blocks, width, total = out_ref.shape
    key_block = pl.program_id(0)
    side = side_ref[0]

    @pl.when(key_block == 0)
    def _():
        @pl.loop(0, blocks)
        def _(block):
            load_rows(q_ref, block, rows_ref, side, scale)
            max_ref[block] = jnp.full((1, total), NEG, f32)
            sum_ref[block] = jnp.zeros((1, total), f32)
            out_ref[block] = jnp.zeros((width, total), f32)

    def work(block, partial):
        keys, values = k_ref[0], v_ref[0]
        spans = [slice(at, at + size) for at, size in column_chunks(total)]
        old_max = [max_ref[block, :, span] for span in spans]
        old_sum = [sum_ref[block, :, span] for span in spans]
        old_out = [out_ref[block, :, span] for span in spans]
        scores = [dot_nt(keys, rows_ref[block, span, :]) for span in spans]
        done = []
        for i, s in enumerate(scores):
            if partial:
                visible = visible_pairs(key_meta_ref, query_meta_ref, block, spans[i])
                s = jnp.where(visible, s, NEG)
            new_max = jnp.maximum(old_max[i], jnp.max(s, 0, keepdims=True))
            weights = jnp.exp(s - new_max)
            if partial:
                weights = jnp.where(visible, weights, 0.0)
            factor = jnp.exp(old_max[i] - new_max)
            new_sum = old_sum[i] * factor + jnp.sum(weights, 0, keepdims=True)
            added = dot_tn(values, weights.astype(jnp.bfloat16))
            done.append((new_max, new_sum, old_out[i] * factor + added))
        for span, (new_max, new_sum, new_out) in zip(spans, done):
            max_ref[block, :, span] = new_max
            sum_ref[block, :, span] = new_sum
            out_ref[block, :, span] = new_out

    @pl.loop(0, blocks)
    def _(block):
        kind = kind_ref[block * blocks + key_block]

        @pl.when(kind == 1)
        def _():
            work(block, False)

        @pl.when(kind == 2)
        def _():
            work(block, True)

    @pl.when(key_block == blocks - 1)
    def _():
        @pl.loop(0, blocks)
        def _(block):
            total_weight = sum_ref[block]
            out = out_ref[block] / total_weight
            out_ref[block] = out
            log_ref[block] = max_ref[block] + jnp.log(total_weight)
            store_rows(window_ref, block, out.T, side)


def attend_back_kernel(
    kind_ref, side_ref, q_ref, k_ref, v_ref, query_meta_ref, key_meta_ref, grad_ref, out_ref, log_ref,
    grad_q_ref, grad_k_ref, grad_v_ref, rows_ref, grad_rows_ref, delta_ref, sum_q_ref, sum_k_ref, sum_v_ref,
    *, scale,
):
    f32, bf16 = jnp.float32, jnp.bfloat16
    blocks, width, total = out_ref.shape
    key_block = pl.program_id(0)
    side = side_ref[0]

    @pl.when(key_block == 0)
    def _():
        @pl.loop(0, blocks)
        def _(block):
            load_rows(q_ref, block, rows_ref, side, scale)
            load_rows(grad_ref, block, grad_rows_ref, side, 1.0)
            grad_rows = grad_rows_ref[block].astype(f32).T
            delta_ref[block] = jnp.sum(grad_rows * out_ref[block], 0, keepdims=True)
            sum_q_ref[block] = jnp.zeros((width, total), f32)

    sum_k_ref[...] = jnp.zeros_like(sum_k_ref)
    sum_v_ref[...] = jnp.zeros_like(sum_v_ref)

    def work(block, partial):
        keys, values = k_ref[0], v_ref[0]
        for at, size in column_chunks(total):
            span = slice(at, at + size)
            q_rows = rows_ref[block, span, :]
            grad_rows = grad_rows_ref[block, span, :]
            prob = jnp.exp(dot_nt(keys, q_rows) - log_ref[block, :, span])
            if partial:
                prob = jnp.where(visible_pairs(key_meta_ref, query_meta_ref, block, span), prob, 0.0)
            grad_prob = dot_nt(values, grad_rows)
            sum_v_ref[...] += dot_nn(prob.astype(bf16), grad_rows)
            grad_score = (prob * (grad_prob - delta_ref[block, :, span])).astype(bf16)
            sum_k_ref[...] += dot_nn(grad_score, q_rows)
            sum_q_ref[block, :, span] += dot_tn(keys, grad_score)

    @pl.loop(0, blocks)
    def _(block):
        kind = kind_ref[block * blocks + key_block]

        @pl.when(kind == 1)
        def _():
            work(block, False)

        @pl.when(kind == 2)
        def _():
            work(block, True)

    grad_k_ref[0] = sum_k_ref[...].astype(bf16)
    grad_v_ref[0] = sum_v_ref[...].astype(bf16)

    @pl.when(key_block == blocks - 1)
    def _():
        @pl.loop(0, blocks)
        def _(block):
            store_rows(grad_q_ref, block, sum_q_ref[block].T * scale, side)


def whole_spec(shape, at=0):
    return pl.BlockSpec(shape, lambda i, *_: (0,) * (len(shape) - 1) + (at,))


def attention_calls(blocks, query_len, key_len, width, lanes, scale, earlier):
    f32, bf16 = jnp.float32, jnp.bfloat16
    total = query_len + query_len // 2
    shape = jax.ShapeDtypeStruct
    q_spec = whole_spec((blocks, query_len, width), lanes[0])
    block_spec = lambda at: pl.BlockSpec((1, key_len, width), lambda i, *_: (i, 0, at))
    metas = [
        whole_spec((blocks, 2, total)),
        pl.BlockSpec((1, key_len, 2), lambda i, *_: (i, 0, 0)),
    ]
    operands = [q_spec, block_spec(lanes[1]), block_spec(lanes[2])] + metas
    window = whole_spec((blocks, query_len, width))
    columns = whole_spec((blocks, width, total))
    logs = whole_spec((blocks, 1, total))
    params = pltpu.CompilerParams(dimension_semantics=("arbitrary",), vmem_limit_bytes=56 * 1024 * 1024)
    pairs = blocks * (blocks + 1) // 2
    product = 2 * total * key_len * width * pairs
    forward = pl.pallas_call(
        functools.partial(attend_kernel, scale=scale),
        grid_spec=pltpu.PrefetchScalarGridSpec(
            num_scalar_prefetch=2,
            grid=(blocks,),
            in_specs=operands,
            out_specs=[window, columns, logs],
            scratch_shapes=[
                pltpu.VMEM((blocks, total, width), bf16),
                pltpu.VMEM((blocks, 1, total), f32),
                pltpu.VMEM((blocks, 1, total), f32),
            ],
        ),
        out_shape=[
            shape((blocks, query_len, width), bf16),
            shape((blocks, width, total), f32),
            shape((blocks, 1, total), f32),
        ],
        compiler_params=params,
        cost_estimate=pl.CostEstimate(
            flops=8 * product, bytes_accessed=16 << 20, transcendentals=total * key_len * pairs
        ),
        name="attend",
    )
    backward = pl.pallas_call(
        leading(functools.partial(attend_back_kernel, scale=scale), 10, earlier),
        grid_spec=pltpu.PrefetchScalarGridSpec(
            num_scalar_prefetch=2,
            grid=(blocks,),
            in_specs=operands + [window, columns, logs] + [ANY_SPEC] * earlier,
            out_specs=[window, block_spec(0), block_spec(0)],
            scratch_shapes=[
                pltpu.VMEM((blocks, total, width), bf16),
                pltpu.VMEM((blocks, total, width), bf16),
                pltpu.VMEM((blocks, 1, total), f32),
                pltpu.VMEM((blocks, width, total), f32),
                pltpu.VMEM((key_len, width), f32),
                pltpu.VMEM((key_len, width), f32),
            ],
        ),
        out_shape=[
            shape((blocks, query_len, width), bf16),
            shape((blocks, key_len, width), bf16),
            shape((blocks, key_len, width), bf16),
        ],
        compiler_params=params,
        cost_estimate=pl.CostEstimate(
            flops=20 * product, bytes_accessed=24 << 20, transcendentals=total * key_len * pairs
        ),
        name="attend_back",
    )
    return forward, backward


def mixed(left, right):
    width = left.shape[1]
    lane = lax.broadcasted_iota(jnp.int32, left.shape, 1)
    return jnp.where(lane < width // 2, pltpu.roll(left, width // 2, 1), pltpu.roll(right, width // 2, 1))


def leading(kernel, count, earlier):
    return lambda *refs: kernel(*refs[:count], *refs[count + earlier :])


def split_kernel(me_ref, rows_ref, *refs, carried):
    outs, windows_ref = refs[carried : carried + HEAD_GROUPS], refs[-1]
    for source, target in zip(refs[:carried], refs[carried + HEAD_GROUPS : -1]):
        target[...] = source[...]
    width = 128
    parts = windows_ref.shape[2] // width
    per_part = rows_ref.shape[1] // parts
    for i in range(parts):
        for t in range(HEAD_GROUPS // 4):
            at = i * per_part + 3 * width * t
            low, middle, high = [
                rows_ref[:, at + m * width : at + (m + 1) * width].astype(jnp.float32) for m in range(3)
            ]
            for g, value in enumerate((low, mixed(low, middle), mixed(middle, high), high)):
                windows_ref[4 * t + g, :, i * width : (i + 1) * width] = value.astype(windows_ref.dtype)
    for k, out in enumerate(outs):
        out[...] = windows_ref[jnp.bitwise_xor(me_ref[0], k)]


def join_kernel(me_ref, *refs):
    f32 = jnp.float32
    ins, (rows_ref, sums_ref, windows_ref) = refs[:HEAD_GROUPS], refs[HEAD_GROUPS:]
    width = 128
    parts = windows_ref.shape[2] // width
    per_part = rows_ref.shape[1] // parts

    @pl.when(pl.program_id(0) == 0)
    def _():
        sums_ref[...] = jnp.zeros_like(sums_ref)

    for k, value_ref in enumerate(ins):
        windows_ref[jnp.bitwise_xor(me_ref[0], k)] = value_ref[...]
    for i in range(parts):
        span = slice(i * width, (i + 1) * width)
        for t in range(HEAD_GROUPS // 4):
            a, b, c, d = [windows_ref[4 * t + g, :, span].astype(f32) for g in range(4)]
            lower = lax.broadcasted_iota(jnp.int32, a.shape, 1) < width // 2
            b, c = pltpu.roll(b, width // 2, 1), pltpu.roll(c, width // 2, 1)
            values = (
                a + jnp.where(lower, 0.0, b),
                jnp.where(lower, b, c),
                jnp.where(lower, c, 0.0) + d,
            )
            for m, value in enumerate(values):
                at = i * per_part + (3 * t + m) * width
                value = value.astype(rows_ref.dtype)
                rows_ref[:, at : at + width] = value
                sums_ref[:, at : at + width] += jnp.sum(value.astype(f32), 0, keepdims=True)


SMEM_SPEC = pl.BlockSpec(memory_space=pltpu.SMEM)
ANY_SPEC = pl.BlockSpec(memory_space=pl.ANY)
VMEM_SPEC = pl.BlockSpec(memory_space=pltpu.VMEM)
LOCAL = pltpu.CompilerParams(vmem_limit_bytes=48 * 1024 * 1024)


def split_rows(me, rows, parts, carried):
    count = rows.shape[0]
    columns = 128 * parts
    outs = pl.pallas_call(
        functools.partial(split_kernel, carried=len(carried)),
        in_specs=[SMEM_SPEC] + [VMEM_SPEC] * (1 + len(carried)),
        out_specs=[VMEM_SPEC] * (HEAD_GROUPS + len(carried)),
        out_shape=[jax.ShapeDtypeStruct((count, columns), rows.dtype)] * HEAD_GROUPS
        + [jax.ShapeDtypeStruct(array.shape, array.dtype) for array in carried],
        scratch_shapes=[pltpu.VMEM((HEAD_GROUPS, count, columns), rows.dtype)],
        compiler_params=LOCAL,
        cost_estimate=pl.CostEstimate(flops=0, bytes_accessed=4 * rows.size * 2, transcendentals=0),
        name="split_rows",
    )(me, rows, *carried)
    return outs[:HEAD_GROUPS], outs[HEAD_GROUPS:]


def add_kernel(kept_ref, received_ref, sum_ref):
    total = kept_ref[...].astype(jnp.float32) + received_ref[...].astype(jnp.float32)
    sum_ref[...] = total.astype(sum_ref.dtype)


def added_after(kept, received, earlier):
    return pl.pallas_call(
        leading(add_kernel, 2, len(earlier)),
        in_specs=[VMEM_SPEC] * 2 + [ANY_SPEC] * len(earlier),
        out_specs=VMEM_SPEC,
        out_shape=jax.ShapeDtypeStruct(kept.shape, kept.dtype),
        compiler_params=LOCAL,
        cost_estimate=pl.CostEstimate(flops=0, bytes_accessed=6 * kept.size, transcendentals=0),
        name="added_after",
    )(kept, received, *earlier)


def pack_kernel(*refs):
    arrays, outs = refs[:-HEAD_GROUPS], refs[-HEAD_GROUPS:]
    for k, out in enumerate(outs):
        for i, array in enumerate(arrays):
            width = array.shape[2]
            out[:, i * width : (i + 1) * width] = array[k]


def pack_rows(arrays, earlier=()):
    blocks, count, width = arrays[0].shape
    shape = jax.ShapeDtypeStruct((count, width * len(arrays)), arrays[0].dtype)
    return pl.pallas_call(
        leading(pack_kernel, len(arrays), len(earlier)),
        in_specs=[VMEM_SPEC] * len(arrays) + [ANY_SPEC] * len(earlier),
        out_specs=[VMEM_SPEC] * blocks,
        out_shape=[shape] * blocks,
        compiler_params=LOCAL,
        cost_estimate=pl.CostEstimate(flops=0, bytes_accessed=4 * blocks * shape.size, transcendentals=0),
        name="pack_rows",
    )(*arrays, *earlier)


def join_rows(me, pieces, model_width, earlier=()):
    count, columns = pieces[0].shape
    total = model_width * columns // 128
    step = count // 4
    return pl.pallas_call(
        leading(join_kernel, 1 + HEAD_GROUPS, len(earlier)),
        grid=(count // step,),
        in_specs=[SMEM_SPEC]
        + [pl.BlockSpec((step, columns), lambda i: (i, 0))] * HEAD_GROUPS
        + [ANY_SPEC] * len(earlier),
        out_specs=[pl.BlockSpec((step, total), lambda i: (i, 0)), pl.BlockSpec((1, total), lambda i: (0, 0))],
        out_shape=[
            jax.ShapeDtypeStruct((count, total), pieces[0].dtype),
            jax.ShapeDtypeStruct((1, total), jnp.float32),
        ],
        scratch_shapes=[pltpu.VMEM((HEAD_GROUPS, step, columns), pieces[0].dtype)],
        compiler_params=LOCAL,
        cost_estimate=pl.CostEstimate(flops=0, bytes_accessed=4 * count * total * 2, transcendentals=0),
        name="join_rows",
    )(me, *pieces, *earlier)


def swapped(pieces, axis):
    length = len(pieces)
    return [pieces[0]] + [
        lax.ppermute(pieces[k], axis, [(i, i ^ k) for i in range(length)]) for k in range(1, length)
    ]


def per_device(
    tokens,
    positions,
    documents,
    ln1_gain,
    ln1_bias,
    w_qkv,
    bias_qv,
    w_out,
    bias_out,
    ln2_gain,
    ln2_bias,
    w_fc,
    bias_fc,
    w_proj,
    bias_proj,
    cotangent,
):
    f32 = jnp.float32
    bf16 = jnp.bfloat16
    seq_count, block_len, model_width = tokens.shape
    head_dim = model_width // HEADS
    width = 2 * head_dim
    score_scale = float(head_dim) ** (-0.5)
    cycle_len = lax.axis_size("ctx")
    owners = lax.axis_size("fsdp")
    me = lax.axis_index("ctx")
    pieces = cycle_len // HEAD_GROUPS
    pair_wise = pieces == 1
    group, piece = me % HEAD_GROUPS, me // HEAD_GROUPS
    side = group % 2
    query_len = block_len // pieces
    half = query_len // 2
    starts = [3 * head_dim * (j // 2) + head_dim * (j % 2) for j in range(HEAD_GROUPS)]
    forward_call, backward_call = attention_calls(
        cycle_len, query_len, block_len, width, (0, 1, 2) if pair_wise else (0, 0, 1), score_scale,
        4 if pair_wise else 0,
    )

    def exchange(value, axis, by):
        return lax.ppermute(value, axis, [(i, i ^ by) for i in range(lax.axis_size(axis))])

    ids = jnp.stack([positions[0], documents[0]])[None]
    if pair_wise:
        by = 1
        while by < cycle_len:
            ids = jnp.concatenate([ids, exchange(ids, "ctx", by)], 0)
            by *= 2
    else:
        ids = lax.all_gather(ids[0], "ctx", axis=0)
    def metas(ids):
        places, docs = ids[:, 0], ids[:, 1]
        first_place, last_place = places[:, 0], places[:, -1]
        first_doc, last_doc = docs[:, 0], docs[:, -1]
        hidden = (
            (first_place[None, :] > last_place[:, None])
            | (last_doc[None, :] < first_doc[:, None])
            | (first_doc[None, :] > last_doc[:, None])
        )
        full = (
            (last_place[None, :] <= first_place[:, None])
            & (first_doc[None, :] == last_doc[:, None])
            & (last_doc[None, :] == first_doc[:, None])
        )
        kinds = jnp.where(hidden, 0, jnp.where(full, 1, 2)).astype(jnp.int32).reshape(-1)
        own_ids = lax.dynamic_slice_in_dim(ids, piece * query_len, query_len, 2)
        shared_ids = lax.dynamic_slice_in_dim(own_ids, side * half, half, 2)
        return kinds, jnp.concatenate([own_ids, shared_ids], 2), jnp.swapaxes(ids, 1, 2)

    side_arg = side.reshape(1).astype(jnp.int32)

    def windows(rows):
        return jnp.stack([rows[:, at : at + width] for at in starts])

    def block_at(stacked, j):
        return lax.dynamic_index_in_dim(stacked, j, 0, keepdims=False)

    def query_pieces(stacked):
        return stacked.reshape(HEAD_GROUPS, pieces, query_len, -1).swapaxes(0, 1).reshape(cycle_len, query_len, -1)

    def over_pieces(stacked):
        return jnp.tile(stacked, (pieces, 1, 1))

    def all_to_all(stacked):
        return lax.all_to_all(stacked, "ctx", 0, 0, tiled=True)

    def joined_queries(back):
        back = back.reshape(pieces, HEAD_GROUPS, query_len, width).swapaxes(0, 1)
        back = back.reshape(HEAD_GROUPS // 2, 2, pieces, 2, half, width)
        lower = back[:, 0, :, 0, :, head_dim:]
        upper = back[:, 1, :, 1, :, :head_dim]
        shared = jnp.stack([lower, upper], 2)
        parts = [back[:, 0, ..., :head_dim], shared, back[:, 1, ..., head_dim:]]
        parts = [part.reshape(HEAD_GROUPS // 2, block_len, head_dim) for part in parts]
        return jnp.concatenate([parts[m][g] for g in range(HEAD_GROUPS // 2) for m in range(3)], 1)

    def joined_keys(back):
        back = back.reshape(pieces, HEAD_GROUPS // 2, 2, block_len, width).astype(f32).sum(0)
        shared = back[:, 0, :, head_dim:] + back[:, 1, :, :head_dim]
        parts = [back[:, 0, :, :head_dim], shared, back[:, 1, :, head_dim:]]
        return jnp.concatenate([parts[m][g] for g in range(HEAD_GROUPS // 2) for m in range(3)], 1).astype(bf16)

    vectors = (ln1_gain, ln1_bias, bias_qv, bias_out, ln2_gain, ln2_bias, bias_fc, bias_proj)
    vector_sizes = [v.size for v in vectors]
    gathered = lax.all_gather(jnp.concatenate(vectors), "fsdp", axis=0).astype(f32)
    cuts = [sum(vector_sizes[:i]) for i in range(len(vectors) + 1)]
    gain_one, shift_one, bqv_all, bout_all, gain_two, shift_two, bfc_all, bproj_all = [
        gathered[:, cuts[i] : cuts[i + 1]].reshape(-1) for i in range(len(vectors))
    ]
    wqkv_all = lax.all_gather(w_qkv, "fsdp", axis=0, tiled=True)
    wfc_all = lax.all_gather(w_fc, "fsdp", axis=0, tiled=True)
    late = lax.all_gather(jnp.concatenate([w_proj, w_out], 0), "fsdp", axis=0)
    wproj_all = late[:, : w_proj.shape[0]].reshape(-1, model_width)
    wout_all = late[:, w_proj.shape[0] :].reshape(-1, model_width)
    me_arg = me.reshape(1).astype(jnp.int32)
    x = tokens.astype(f32).reshape(-1, model_width)
    normed_one, inverse_one = norm_stats(x)
    h_one = (normed_one * gain_one + shift_one).astype(bf16)
    bias_all = jnp.concatenate(
        [bqv_all[:model_width], jnp.zeros((model_width,), f32), bqv_all[model_width:]]
    )
    qkv = (jnp.dot(h_one, wqkv_all, preferred_element_type=f32) + bias_all).astype(bf16)
    if pair_wise:
        parts, (ids,) = split_rows(me_arg, qkv, 3, (ids,))
        taken = jnp.stack(swapped(parts, "ctx"))
        operands = (taken, taken, taken)
    else:
        q_windows, k_windows, v_windows = [
            windows(qkv[:, i * model_width : (i + 1) * model_width]) for i in range(3)
        ]
        taken_q = all_to_all(query_pieces(q_windows))
        taken_kv = all_to_all(over_pieces(jnp.concatenate([k_windows, v_windows], -1)))
        operands = (taken_q, taken_kv, taken_kv)
    kinds, query_meta, key_meta = metas(ids)
    operands = (kinds, side_arg) + operands + (query_meta, key_meta)
    out_windows, out_columns, log_total = forward_call(*operands)
    cot_rows = cotangent.reshape(-1, model_width)
    grad_act = jnp.einsum("td,fd->tf", cot_rows, wproj_all, preferred_element_type=f32)
    if pair_wise:
        back = swapped([out_windows[k] for k in range(cycle_len)], "ctx")
        attended_low, _ = join_rows(me_arg, back, model_width, (wproj_all, wout_all, grad_act))
    else:
        attended_low = joined_queries(all_to_all(out_windows))
    x_two = x + jnp.dot(attended_low, wout_all, preferred_element_type=f32) + bout_all
    normed_two, inverse_two = norm_stats(x_two)
    h_two = (normed_two * gain_two + shift_two).astype(bf16)
    pre_act = jnp.dot(h_two, wfc_all, preferred_element_type=f32) + bfc_all
    activated, gelu_pull = jax.vjp(lambda t: jax.nn.gelu(t, approximate=True), pre_act)
    activated_low = activated.astype(bf16)
    result = x_two + jnp.dot(activated_low, wproj_all, preferred_element_type=f32) + bproj_all
    block_out = result.astype(bf16).reshape(tokens.shape)
    grad_y = cot_rows.astype(f32)
    grad_bproj = jnp.sum(grad_y, 0)
    grad_pre = gelu_pull(grad_act)[0].astype(bf16)
    grad_bfc = jnp.sum(grad_pre.astype(f32), 0)
    grad_h_two = jnp.einsum("tf,df->td", grad_pre, wfc_all, preferred_element_type=f32)
    grad_g_two = jnp.sum(grad_h_two * normed_two, 0)
    grad_b_two = jnp.sum(grad_h_two, 0)
    grad_x_two = grad_y + norm_back(grad_h_two, normed_two, inverse_two, gain_two)
    grad_branch = grad_x_two.astype(bf16)
    grad_bout = jnp.sum(grad_branch.astype(f32), 0)
    grad_att = jnp.einsum("te,de->td", grad_branch, wout_all, preferred_element_type=f32).astype(bf16)
    row, column = me // 2, me % 2
    chip, core = lax.axis_index("fsdp") // 2, lax.axis_index("fsdp") % 2
    rows_apart = cycle_len // 2

    def pick(value, j, axis):
        return lax.dynamic_index_in_dim(value, j, axis, keepdims=False)

    def added(kept, *others):
        total = kept.astype(f32)
        for other in others:
            total = total + other.astype(f32)
        return total.astype(bf16)

    def product(left, right):
        grad = jnp.einsum("tr,tc->rc", left, right, preferred_element_type=f32).astype(bf16)
        return grad.reshape(owners // 2, 2, -1, grad.shape[1])

    def over_cores(grad):
        return added(pick(grad, core, 1), exchange(pick(grad, 1 - core, 1), "fsdp", 1))

    def first_parts(a, b):
        b = b.reshape(2, rows_apart, 2, -1, b.shape[-1])
        return (pick(a, chip, 0), pick(b, column, 2)), (pick(a, 1 - chip, 0), pick(b, 1 - column, 2))

    def second_parts(kept, sent, earlier=()):
        a = added_after(kept[0], exchange(sent[0], "fsdp", 2), earlier)
        b = added_after(kept[1], exchange(sent[1], "ctx", 1), earlier)
        a = a.reshape(rows_apart, 2, -1, a.shape[-1])
        return (pick(a, column, 1), pick(b, chip, 0)), (pick(a, 1 - column, 1), pick(b, 1 - chip, 0))

    def third_parts(kept, sent, earlier=()):
        a = added_after(kept[0], exchange(sent[0], "ctx", 1), earlier)
        return a, added_after(kept[1], exchange(sent[1], "fsdp", 2), earlier)

    def last_sum(value):
        return added(
            pick(value, row, 0), *[exchange(pick(value, row ^ k, 0), "ctx", 2 * k) for k in range(1, rows_apart)]
        )

    def spread(mine):
        around = jnp.stack([mine] + [exchange(mine, "ctx", 2 * k) for k in range(1, rows_apart)])
        around = jnp.stack([pick(around, row ^ j, 0) for j in range(rows_apart)])
        both = jnp.stack([around, exchange(around, "ctx", 1)])
        both = jnp.stack([pick(both, column ^ j, 0) for j in range(2)], 1)
        return both.reshape(-1, mine.shape[-1])

    def over_ctx(pair):
        own = added(pick(pair, chip, 0), exchange(pick(pair, 1 - chip, 0), "fsdp", 2))
        mine = lax.psum_scatter(own, "ctx", scatter_dimension=0, tiled=True)
        return lax.all_gather(mine, "ctx", axis=0, tiled=True)

    def early_sums(cot_rows, h_two, attended_low):
        early = [
            over_cores(product(left, right))
            for left, right in ((activated_low, cot_rows), (h_two, grad_pre), (attended_low, grad_branch))
        ]
        return early[0], jnp.concatenate(early[1:], -1)

    if pair_wise:
        parts, carried = split_rows(me_arg, grad_att, 1, (cot_rows, h_two, attended_low))
        taken_grad = jnp.stack(swapped(parts, "ctx"))
        early = first_parts(*early_sums(*carried))
        earlier = (*early[0], *early[1])
    else:
        taken_grad = all_to_all(query_pieces(windows(grad_att)))
        early = [over_ctx(pair) for pair in early_sums(cot_rows, h_two, attended_low)]
        earlier = ()

    grad_q_windows, grad_k_windows, grad_v_windows = backward_call(
        *operands, taken_grad, out_columns, log_total, *earlier
    )
    if pair_wise:
        back = swapped(pack_rows((grad_q_windows, grad_k_windows, grad_v_windows)), "ctx")
        early = second_parts(*early, (grad_q_windows,))
        grad_qkv, grad_sums = join_rows(me_arg, back, model_width)
        early = [spread(last_sum(value)) for value in third_parts(*early, (grad_qkv,))]
        grad_sums = grad_sums[0]
    else:
        back_q = all_to_all(grad_q_windows)
        back_kv = all_to_all(jnp.concatenate([grad_k_windows, grad_v_windows], -1))
        grad_k_low, grad_v_low = joined_keys(back_kv[..., :width]), joined_keys(back_kv[..., width:])
        grad_qkv = jnp.concatenate([joined_queries(back_q), grad_k_low, grad_v_low], -1)
        grad_sums = jnp.sum(grad_qkv.astype(f32), 0)
    grad_bqv = jnp.concatenate([grad_sums[:model_width], grad_sums[2 * model_width :]])
    grad_h_one = jnp.einsum("te,de->td", grad_qkv, wqkv_all, preferred_element_type=f32)
    grad_g_one = jnp.sum(grad_h_one * normed_one, 0)
    grad_b_one = jnp.sum(grad_h_one, 0)
    grad_x = grad_x_two + norm_back(grad_h_one, normed_one, inverse_one, gain_one)
    grad_tokens = grad_x.astype(bf16).reshape(tokens.shape)

    vector_grads = (grad_g_one, grad_b_one, grad_bqv, grad_bout, grad_g_two, grad_b_two, grad_bfc, grad_bproj)
    packed = jnp.concatenate([grad.reshape(owners, -1) for grad in vector_grads], 1).astype(bf16)
    own_rows = w_qkv.shape[0]
    extra = -(-packed.shape[1] // (own_rows * 128)) * 128
    packed = jnp.pad(packed, ((0, 0), (0, own_rows * extra - packed.shape[1])))
    packed = packed.reshape(owners // 2, 2, own_rows, extra)
    last = over_cores(jnp.concatenate([product(h_one, grad_qkv), packed], -1))
    if pair_wise:
        cut = w_qkv.shape[1] // 256 * 128
        last = third_parts(*second_parts(*first_parts(last[..., :cut], last[..., cut:])))
        last = spread(last_sum(jnp.concatenate(last, -1)))
    else:
        last = over_ctx(last)
    last = last.astype(f32)
    early = [value.astype(f32) for value in early]
    reduced_wproj = early[0]
    reduced_wfc, reduced_wout = early[1][:, : w_fc.shape[1]], early[1][:, w_fc.shape[1] :]
    reduced_wqkv = last[:, : w_qkv.shape[1]]
    reduced_vectors = last[:, w_qkv.shape[1] :].reshape(-1)
    pieces_of = [reduced_vectors[cuts[i] : cuts[i + 1]] for i in range(len(vectors))]
    g_one, b_one, g_bqv, g_bout, g_two, b_two, g_bfc, g_bproj = pieces_of
    return (
        block_out,
        grad_tokens,
        g_one,
        b_one,
        reduced_wqkv,
        g_bqv,
        reduced_wout,
        g_bout,
        g_two,
        b_two,
        reduced_wfc,
        g_bfc,
        reduced_wproj,
        g_bproj,
    )


def solution(mesh):
    return jax.shard_map(
        per_device,
        mesh=mesh,
        in_specs=(
            P("fsdp", "ctx", None),
            P("fsdp", "ctx"),
            P("fsdp", "ctx"),
            P("fsdp"),
            P("fsdp"),
            P("fsdp", None),
            P("fsdp"),
            P("fsdp", None),
            P("fsdp"),
            P("fsdp"),
            P("fsdp"),
            P("fsdp", None),
            P("fsdp"),
            P("fsdp", None),
            P("fsdp"),
            P("fsdp", "ctx", None),
        ),
        out_specs=(
            P("fsdp", "ctx", None),
            P("fsdp", "ctx", None),
            P("fsdp"),
            P("fsdp"),
            P("fsdp", None),
            P("fsdp"),
            P("fsdp", None),
            P("fsdp"),
            P("fsdp"),
            P("fsdp"),
            P("fsdp", None),
            P("fsdp"),
            P("fsdp", None),
            P("fsdp"),
        ),
        check_vma=False,
    )
```
